32 devices in a mesh: dp: 4 (over y, x), fsdp: 8 (over z, core).
Axes of the slice: x: 2, y: 2, z: 4, core: 2. Of those that a mesh axis runs over, the one named last changes fastest.
Arguments:
- tokens: bfloat16 [4096, 768], P(('dp', 'fsdp')), may hold values from -24 to 24
- lengths: int32 [32], P(('dp', 'fsdp')), may hold values from 1 to 128, 2560 in all
- cotangent: float32 [4096, 768], P(('dp', 'fsdp')), may hold values from -6 to 6
- query_weight: bfloat16 [768, 768], P(('dp', 'fsdp')), may hold values from -0.21875 to 0.21875
- query_bias: bfloat16 [768], P(('dp', 'fsdp')), may hold values from -3 to 3
- key_weight: bfloat16 [768, 768], P(('dp', 'fsdp')), may hold values from -0.21875 to 0.21875
- value_weight: bfloat16 [768, 768], P(('dp', 'fsdp')), may hold values from -0.21875 to 0.21875
- value_bias: bfloat16 [768], P(('dp', 'fsdp')), may hold values from -3 to 3
- out_weight: bfloat16 [768, 768], P(('dp', 'fsdp')), may hold values from -0.875 to 0.875
- out_bias: bfloat16 [768], P(('dp', 'fsdp')), may hold values from -3 to 3
- norm1_gain: bfloat16 [768], P(('dp', 'fsdp')), may hold values from 0.5 to 1.5
- norm1_shift: bfloat16 [768], P(('dp', 'fsdp')), may hold values from -3 to 3
- inner_weight: bfloat16 [768, 3072], P(('dp', 'fsdp')), may hold values from -0.21875 to 0.21875
- inner_bias: bfloat16 [3072], P(('dp', 'fsdp')), may hold values from -3 to 3
- outer_weight: bfloat16 [3072, 768], P(('dp', 'fsdp')), may hold values from -0.109375 to 0.109375
- outer_bias: bfloat16 [768], P(('dp', 'fsdp')), may hold values from -3 to 3
- norm2_gain: bfloat16 [768], P(('dp', 'fsdp')), may hold values from 0.5 to 1.5
- norm2_shift: bfloat16 [768], P(('dp', 'fsdp')), may hold values from -3 to 3
Outputs:
- layer_out: float32 [4096, 768], P(('dp', 'fsdp'))
- grad_tokens: float32 [4096, 768], P(('dp', 'fsdp'))
- grad_query_weight: float32 [768, 768], P(('dp', 'fsdp'))
- grad_query_bias: float32 [768], P(('dp', 'fsdp'))
- grad_key_weight: float32 [768, 768], P(('dp', 'fsdp'))
- grad_value_weight: float32 [768, 768], P(('dp', 'fsdp'))
- grad_value_bias: float32 [768], P(('dp', 'fsdp'))
- grad_out_weight: float32 [768, 768], P(('dp', 'fsdp'))
- grad_out_bias: float32 [768], P(('dp', 'fsdp'))
- grad_norm1_gain: float32 [768], P(('dp', 'fsdp'))
- grad_norm1_shift: float32 [768], P(('dp', 'fsdp'))
- grad_inner_weight: float32 [768, 3072], P(('dp', 'fsdp'))
- grad_inner_bias: float32 [3072], P(('dp', 'fsdp'))
- grad_outer_weight: float32 [3072, 768], P(('dp', 'fsdp'))
- grad_outer_bias: float32 [768], P(('dp', 'fsdp'))
- grad_norm2_gain: float32 [768], P(('dp', 'fsdp'))
- grad_norm2_shift: float32 [768], P(('dp', 'fsdp'))
The draws below stay inside these ranges and needn't reach their ends.
Inputs may be any that keep to these rules, and one draw needn't show every extreme that they name: lengths sum to 2560 and the longest is exactly 128.
All inputs are finite; a program needn't handle non-finite values. No bound on the sum of `lengths` on one device may be relied on, other than what follows from the above.
Results may differ from the reference program's by a relative error of at most 0.013.
Values may be sent and summed in bfloat16 or wider, within the bound.
A program may use at most 192 MiB of HBM per device.

```python
import math
import jax
import jax.numpy as jnp
import numpy as np
from jax import lax

D = 768
HEADS = 12
HEAD_DIM = 64
FF = 3072
L = 128
SEQS = 32
TOKENS = 4096


def draw_tokens(key, part):
    entry_key = jax.random.fold_in(key, 11)
    pairing_key = jax.random.fold_in(key, 23)
    entries = jax.random.truncated_normal(entry_key, -6.0, 6.0, (TOKENS, D), jnp.float32)
    pairing = jax.random.permutation(pairing_key, SEQS).astype(jnp.int32)
    block_width = D // SEQS
    column_block = jnp.arange(D, dtype=jnp.int32) // block_width
    row_sequence = jnp.arange(TOKENS, dtype=jnp.int32) // L
    first_block = pairing[row_sequence]
    second_block = pairing[(row_sequence + SEQS // 2) % SEQS]
    spiked_cell = (column_block[None, :] == first_block[:, None]) | (column_block[None, :] == second_block[:, None])
    spiked = entries * jnp.where(spiked_cell, 4.0, 1.0)
    return spiked.astype(jnp.bfloat16)


def shard_levels(key, extent, split, smallest, top_value):
    level, own = 1.0, jax.random.fold_in(key, 6)
    for axis_at, blocks in split:
        heights = jnp.exp(jax.random.uniform(jax.random.fold_in(own, axis_at), (blocks,), jnp.float32, smallest / len(split), top_value / len(split)))
        level = level * jnp.repeat(heights, extent[axis_at] // blocks).reshape([-1 if axis == axis_at else 1 for axis in range(len(extent))])
    return level


def split_up(count, total, limit, lean):
    weights = [(1 << 20) // math.isqrt(rank ** lean) + 1 for rank in range(2, count + 1)]
    spare, holding = total - limit - (count - 1), [1] * (count - 1)
    while spare > 0:
        movable = [i for i in range(count - 1) if holding[i] < limit]
        whole, left = sum([weights[i] for i in movable]), spare
        for i in movable:
            addition = min(limit - holding[i], max(1, left * weights[i] // whole), spare)
            holding[i] = holding[i] + addition
            spare = spare - addition
    return np.array([limit] + holding)


def uneven_parts(own_key, number_of, total, most, lean):
    if number_of == 2:
        one = jax.random.randint(own_key, (), max(1, total - most), min(most, total - 1) + 1)
        return jnp.stack([one, total - one])
    sizes = jnp.asarray(split_up(number_of, total, most, lean), jnp.int32)
    couples = (number_of - 1) // 2
    source_of, taker = sizes[1:1 + 2 * couples:2], sizes[2:2 + 2 * couples:2]
    margin = jnp.minimum(source_of - 1, most - taker)
    passed = jax.random.randint(jax.random.fold_in(own_key, 1), (couples,), 0, 1 << 20) % (margin + 1)
    sizes = sizes.at[1:1 + 2 * couples:2].set(source_of - passed).at[2:2 + 2 * couples:2].set(taker + passed)
    return sizes[jax.random.permutation(jax.random.fold_in(own_key, 2), number_of)]


def noise(stream_key, extent, deviation, bound, shards=(), held_as=jnp.bfloat16):
    values = jax.random.normal(stream_key, extent, jnp.float32) * deviation
    if len(shards) > 0:
        values = shard_levels(stream_key, extent, shards, -0.22, 0.18) * values
    return jnp.clip(values, min=-bound, max=bound).astype(held_as)


def setup_inputs(seed: int = 0) -> dict:
    arg_keys = jax.random.split(jax.random.key(seed), 19)
    tokens = draw_tokens(jax.random.fold_in(arg_keys[18], 71), 0)
    lengths = uneven_parts(arg_keys[1], SEQS, SEQS * L * 5 // 8, L, 2).astype(jnp.int32)
    cotangent = noise(arg_keys[2], (TOKENS, D), 1.0, 6.0, ((0, 32),), jnp.float32)
    query_weight = noise(arg_keys[3], (D, D), D ** -0.5, 0.21875, ((0, 32),))
    query_bias = noise(arg_keys[4], (D,), 0.5, 3.0, ((0, 32),))
    key_weight = noise(arg_keys[5], (D, D), D ** -0.5, 0.21875, ((0, 32),))
    value_weight = noise(arg_keys[6], (D, D), D ** -0.5, 0.21875, ((0, 32),))
    value_bias = noise(arg_keys[7], (D,), 0.5, 3.0, ((0, 32),))
    out_weight = noise(arg_keys[8], (D, D), (D // 16) ** -0.5, 0.875, ((0, 32),))
    out_bias = noise(arg_keys[9], (D,), 0.5, 3.0, ((0, 32),))
    norm1_gain = jnp.clip(1.0 + 0.1 * jax.random.normal(arg_keys[10], (D,), jnp.float32), 0.5, 1.5).astype(jnp.bfloat16)
    norm1_shift = noise(arg_keys[11], (D,), 0.5, 3.0, ((0, 32),))
    inner_weight = noise(arg_keys[12], (D, FF), D ** -0.5, 0.21875, ((0, 32),))
    inner_bias = noise(arg_keys[13], (FF,), 0.5, 3.0, ((0, 32),))
    outer_weight = noise(arg_keys[14], (FF, D), FF ** -0.5, 0.109375, ((0, 32),))
    outer_bias = noise(arg_keys[15], (D,), 0.5, 3.0, ((0, 32),))
    norm2_gain = jnp.clip(1.0 + 0.1 * jax.random.normal(arg_keys[16], (D,), jnp.float32), 0.5, 1.5).astype(jnp.bfloat16)
    norm2_shift = noise(arg_keys[17], (D,), 0.5, 3.0, ((0, 32),))
    return dict(tokens=tokens, lengths=lengths, cotangent=cotangent, query_weight=query_weight, query_bias=query_bias, key_weight=key_weight, value_weight=value_weight, value_bias=value_bias, out_weight=out_weight, out_bias=out_bias, norm1_gain=norm1_gain, norm1_shift=norm1_shift, inner_weight=inner_weight, inner_bias=inner_bias, outer_weight=outer_weight, outer_bias=outer_bias, norm2_gain=norm2_gain, norm2_shift=norm2_shift)


NORM_EPS = 1e-12
ATTN_SCALE = 0.125

def layer_norm(summed, gain, shift):
    center = summed - lax.optimization_barrier(jnp.mean(summed, -1, keepdims=True))
    rstd = lax.rsqrt(lax.optimization_barrier(jnp.mean(center * center, -1, keepdims=True)) + NORM_EPS)
    normed = center * rstd
    return (normed * gain.astype(jnp.float32) + shift.astype(jnp.float32), normed, rstd)

def norm_back(grad_in, normed, rstd, gain):
    scaled = grad_in * gain.astype(jnp.float32)
    return rstd * (scaled - lax.optimization_barrier(jnp.mean(scaled, -1, keepdims=True)) - normed * lax.optimization_barrier(jnp.mean(scaled * normed, -1, keepdims=True)))

def gelu_parts(pre):
    cdf = 0.5 * (1.0 + jax.scipy.special.erf(pre * 0.7071067811865476))
    slope = cdf + pre * jnp.exp(-0.5 * pre * pre) * 0.3989422804014327
    return (pre * cdf, slope)

def heads_of(rows):
    return rows.reshape(rows.shape[0], HEADS, HEAD_DIM).astype(jnp.float32)

def get_scores(query, keys, length):
    scores = jnp.einsum('qhd,khd->hqk', heads_of(query), heads_of(keys)) * ATTN_SCALE
    valid = jnp.arange(scores.shape[-1]).astype(jnp.int32) < length
    return jnp.where(valid[None, None, :], scores, -1e+30)

def one_sequence(tokens, cotangent, length, weights):
    query_weight, query_bias, key_weight, value_weight, value_bias, out_weight, out_bias, norm1_gain, norm1_shift, inner_weight, inner_bias, outer_weight, outer_bias, norm2_gain, norm2_shift = weights
    f32 = jnp.float32
    bf16 = jnp.bfloat16
    query = (jnp.dot(tokens, query_weight, preferred_element_type=f32) + query_bias.astype(f32)).astype(bf16)
    keys = jnp.dot(tokens, key_weight, preferred_element_type=f32).astype(bf16)
    values = (jnp.dot(tokens, value_weight, preferred_element_type=f32) + value_bias.astype(f32)).astype(bf16)
    scores = get_scores(query, keys, length)
    top = lax.optimization_barrier(jnp.max(scores, -1))
    lse = top + jnp.log(lax.optimization_barrier(jnp.sum(jnp.exp(scores - top[..., None]), -1)))
    probs = jnp.exp(scores - lse[..., None])
    probs_b = probs.astype(bf16)
    mixed = jnp.einsum('hqk,khd->qhd', probs_b.astype(f32), heads_of(values))
    mixed = mixed.reshape(tokens.shape[0], -1).astype(bf16)
    first_sum = tokens.astype(f32) + jnp.dot(mixed, out_weight, preferred_element_type=f32) + out_bias.astype(f32)
    hidden, normed_one, rstd_one = layer_norm(first_sum, norm1_gain, norm1_shift)
    hidden_b = hidden.astype(bf16)
    pre = jnp.dot(hidden_b, inner_weight, preferred_element_type=f32) + inner_bias.astype(f32)
    act, slope = gelu_parts(pre)
    act_b = act.astype(bf16)
    second_sum = hidden + jnp.dot(act_b, outer_weight, preferred_element_type=f32) + outer_bias.astype(f32)
    layer_out, normed_two, rstd_two = layer_norm(second_sum, norm2_gain, norm2_shift)
    d_second = norm_back(cotangent, normed_two, rstd_two, norm2_gain)
    d_second_b = d_second.astype(bf16)
    d_pre = jnp.dot(d_second_b, outer_weight.T, preferred_element_type=f32) * slope
    d_pre_b = d_pre.astype(bf16)
    d_hidden = d_second + jnp.dot(d_pre_b, inner_weight.T, preferred_element_type=f32)
    d_first = norm_back(d_hidden, normed_one, rstd_one, norm1_gain)
    d_first_b = d_first.astype(bf16)
    d_mixed = jnp.dot(d_first_b, out_weight.T, preferred_element_type=f32).astype(bf16)
    again = jnp.exp(get_scores(query, keys, length) - lse[..., None])
    again_b = again.astype(bf16)
    d_probs = jnp.einsum('qhd,khd->hqk', heads_of(d_mixed), heads_of(values))
    d_values_f = jnp.einsum('hqk,qhd->khd', again_b.astype(f32), heads_of(d_mixed)).reshape(tokens.shape[0], -1)
    delta = lax.optimization_barrier(jnp.sum(again * d_probs, -1, keepdims=True))
    d_scores = (again * (d_probs - delta) * ATTN_SCALE).astype(bf16).astype(f32)
    d_query_f = jnp.einsum('hqk,khd->qhd', d_scores, heads_of(keys)).reshape(tokens.shape[0], -1)
    d_keys_f = jnp.einsum('hqk,qhd->khd', d_scores, heads_of(query)).reshape(tokens.shape[0], -1)
    d_query = d_query_f.astype(bf16)
    d_keys = d_keys_f.astype(bf16)
    d_values = d_values_f.astype(bf16)
    grad_tokens = d_first + jnp.dot(d_query, query_weight.T, preferred_element_type=f32) + jnp.dot(d_keys, key_weight.T, preferred_element_type=f32) + jnp.dot(d_values, value_weight.T, preferred_element_type=f32)
    grads = (jnp.dot(tokens.T, d_query, preferred_element_type=f32), lax.optimization_barrier(jnp.sum(d_query_f, 0)), jnp.dot(tokens.T, d_keys, preferred_element_type=f32), jnp.dot(tokens.T, d_values, preferred_element_type=f32), lax.optimization_barrier(jnp.sum(d_values_f, 0)), jnp.dot(mixed.T, d_first_b, preferred_element_type=f32), lax.optimization_barrier(jnp.sum(d_first, 0)), lax.optimization_barrier(jnp.sum(d_hidden * normed_one, 0)), lax.optimization_barrier(jnp.sum(d_hidden, 0)), jnp.dot(hidden_b.T, d_pre_b, preferred_element_type=f32), lax.optimization_barrier(jnp.sum(d_pre, 0)), jnp.dot(act_b.T, d_second_b, preferred_element_type=f32), lax.optimization_barrier(jnp.sum(d_second, 0)), lax.optimization_barrier(jnp.sum(cotangent * normed_two, 0)), lax.optimization_barrier(jnp.sum(cotangent, 0)))
    return (layer_out, grad_tokens, grads)

def reference(tokens, lengths, cotangent, query_weight, query_bias, key_weight, value_weight, value_bias, out_weight, out_bias, norm1_gain, norm1_shift, inner_weight, inner_bias, outer_weight, outer_bias, norm2_gain, norm2_shift):
    weights = (query_weight, query_bias, key_weight, value_weight, value_bias, out_weight, out_bias, norm1_gain, norm1_shift, inner_weight, inner_bias, outer_weight, outer_bias, norm2_gain, norm2_shift)
    token_seqs = tokens.reshape(SEQS, L, D)
    cot_seqs = cotangent.reshape(SEQS, L, D)
    start = tuple((jnp.zeros(w.shape, jnp.float32) for w in weights))

    def step(totals, items):
        rows, cot_rows, length = items
        out_rows, grad_rows, grads = one_sequence(rows, cot_rows, length, weights)
        return (tuple((a + b for a, b in zip(totals, grads))), (out_rows, grad_rows))
    totals, (outs, grad_outs) = lax.scan(step, start, (token_seqs, cot_seqs, lengths))
    factor = 1.0 / jnp.sqrt(jnp.float32(TOKENS))
    scaled = tuple((g * factor for g in totals))
    return (outs.reshape(TOKENS, D), grad_outs.reshape(TOKENS, D), scaled[0], scaled[1], scaled[2], scaled[3], scaled[4], scaled[5], scaled[6], scaled[7], scaled[8], scaled[9], scaled[10], scaled[11], scaled[12], scaled[13], scaled[14])
```

```python
import jax
import jax.numpy as jnp
from jax import lax
from jax.sharding import PartitionSpec as P

D = 768
HEADS = 12
HEAD_DIM = 64
FF = 3072


NORM_EPS = 1e-12
ATTN_SCALE = 0.125


def layer_norm(summed, gain, shift):
    center = summed - jnp.mean(summed, -1, keepdims=True)
    rstd = lax.rsqrt(jnp.mean(center * center, -1, keepdims=True) + NORM_EPS)
    normed = center * rstd
    return (normed * gain.astype(jnp.float32) + shift.astype(jnp.float32), normed, rstd)


def norm_back(grad_in, normed, rstd, gain):
    scaled = grad_in * gain.astype(jnp.float32)
    return rstd * (
        scaled
        - jnp.mean(scaled, -1, keepdims=True)
        - normed * jnp.mean(scaled * normed, -1, keepdims=True)
    )


def gelu_parts(pre):
    cdf = 0.5 * (1.0 + jax.scipy.special.erf(pre * 0.7071067811865476))
    slope = cdf + pre * jnp.exp(-0.5 * pre * pre) * 0.3989422804014327
    return (pre * cdf, slope)


def heads_of(rows):
    return rows.reshape(rows.shape[0], HEADS, HEAD_DIM)


def get_scores(query, keys, length):
    scores = (
        jnp.einsum(
            "qhd,khd->hqk", heads_of(query), heads_of(keys), preferred_element_type=jnp.float32
        )
        * ATTN_SCALE
    )
    valid = jnp.arange(scores.shape[-1]) < length
    return jnp.where(valid[None, None, :], scores, -1e30)


def forward_pass(tokens, length, weights):
    (
        query_weight,
        query_bias,
        key_weight,
        value_weight,
        value_bias,
        out_weight,
        out_bias,
        norm1_gain,
        norm1_shift,
        inner_weight,
        inner_bias,
        outer_weight,
        outer_bias,
        norm2_gain,
        norm2_shift,
    ) = weights
    f32 = jnp.float32
    bf16 = jnp.bfloat16
    query = (
        jnp.dot(tokens, query_weight, preferred_element_type=f32) + query_bias.astype(f32)
    ).astype(bf16)
    keys = jnp.dot(tokens, key_weight, preferred_element_type=f32).astype(bf16)
    values = (
        jnp.dot(tokens, value_weight, preferred_element_type=f32) + value_bias.astype(f32)
    ).astype(bf16)
    scores = get_scores(query, keys, length)
    top = jnp.max(scores, -1)
    lse = top + jnp.log(jnp.sum(jnp.exp(scores - top[..., None]), -1))
    probs_b = jnp.exp(scores - lse[..., None]).astype(bf16)
    mixed = jnp.einsum("hqk,khd->qhd", probs_b, heads_of(values), preferred_element_type=f32)
    mixed = mixed.reshape(tokens.shape[0], -1).astype(bf16)
    first_sum = (
        tokens.astype(f32)
        + jnp.dot(mixed, out_weight, preferred_element_type=f32)
        + out_bias.astype(f32)
    )
    hidden, normed_one, rstd_one = layer_norm(first_sum, norm1_gain, norm1_shift)
    hidden_b = hidden.astype(bf16)
    pre = jnp.dot(hidden_b, inner_weight, preferred_element_type=f32) + inner_bias.astype(f32)
    act, slope = gelu_parts(pre)
    act_b = act.astype(bf16)
    second_sum = (
        hidden + jnp.dot(act_b, outer_weight, preferred_element_type=f32) + outer_bias.astype(f32)
    )
    layer_out, normed_two, rstd_two = layer_norm(second_sum, norm2_gain, norm2_shift)
    saved = (
        query,
        keys,
        values,
        lse,
        mixed,
        normed_one,
        rstd_one,
        hidden_b,
        slope,
        act_b,
        normed_two,
        rstd_two,
    )
    return (layer_out, saved)


def backward_pass(tokens, cotangent, length, weights, saved):
    (
        query_weight,
        query_bias,
        key_weight,
        value_weight,
        value_bias,
        out_weight,
        out_bias,
        norm1_gain,
        norm1_shift,
        inner_weight,
        inner_bias,
        outer_weight,
        outer_bias,
        norm2_gain,
        norm2_shift,
    ) = weights
    (
        query,
        keys,
        values,
        lse,
        mixed,
        normed_one,
        rstd_one,
        hidden_b,
        slope,
        act_b,
        normed_two,
        rstd_two,
    ) = saved
    f32 = jnp.float32
    bf16 = jnp.bfloat16
    d_second = norm_back(cotangent, normed_two, rstd_two, norm2_gain)
    d_second_b = d_second.astype(bf16)
    d_pre = jnp.dot(d_second_b, outer_weight.T, preferred_element_type=f32) * slope
    d_pre_b = d_pre.astype(bf16)
    d_hidden = d_second + jnp.dot(d_pre_b, inner_weight.T, preferred_element_type=f32)
    d_first = norm_back(d_hidden, normed_one, rstd_one, norm1_gain)
    d_first_b = d_first.astype(bf16)
    d_mixed = jnp.dot(d_first_b, out_weight.T, preferred_element_type=f32).astype(bf16)
    again = jnp.exp(get_scores(query, keys, length) - lse[..., None])
    again_b = again.astype(bf16)
    d_probs = jnp.einsum(
        "qhd,khd->hqk", heads_of(d_mixed), heads_of(values), preferred_element_type=f32
    )
    d_values_f = jnp.einsum(
        "hqk,qhd->khd", again_b, heads_of(d_mixed), preferred_element_type=f32
    ).reshape(tokens.shape[0], -1)
    delta = jnp.sum(again * d_probs, -1, keepdims=True)
    d_scores = (again * (d_probs - delta) * ATTN_SCALE).astype(bf16)
    d_query_f = jnp.einsum(
        "hqk,khd->qhd", d_scores, heads_of(keys), preferred_element_type=f32
    ).reshape(tokens.shape[0], -1)
    d_keys_f = jnp.einsum(
        "hqk,qhd->khd", d_scores, heads_of(query), preferred_element_type=f32
    ).reshape(tokens.shape[0], -1)
    d_query = d_query_f.astype(bf16)
    d_keys = d_keys_f.astype(bf16)
    d_values = d_values_f.astype(bf16)
    grad_tokens = (
        d_first
        + jnp.dot(d_query, query_weight.T, preferred_element_type=f32)
        + jnp.dot(d_keys, key_weight.T, preferred_element_type=f32)
        + jnp.dot(d_values, value_weight.T, preferred_element_type=f32)
    )
    small = (
        jnp.sum(d_query_f, 0),
        jnp.sum(d_values_f, 0),
        jnp.sum(d_first, 0),
        jnp.sum(d_hidden * normed_one, 0),
        jnp.sum(d_hidden, 0),
        jnp.sum(d_pre, 0),
        jnp.sum(d_second, 0),
        jnp.sum(cotangent * normed_two, 0),
        jnp.sum(cotangent, 0),
    )
    factors = (
        tokens,
        d_query,
        d_keys,
        d_values,
        mixed,
        d_first_b,
        hidden_b,
        d_pre_b,
        act_b,
        d_second_b,
    )
    return (grad_tokens, small, factors)


def round_up(value, multiple):
    return -(-value // multiple) * multiple


def to_row(vectors, dtype):
    flat = jnp.concatenate([v.astype(dtype) for v in vectors], -1)
    lead = flat.shape[:-1]
    pad = [(0, 0)] * len(lead) + [(0, D - flat.shape[-1])]
    return jnp.pad(flat, pad).reshape(lead + (1, D))


def gather_rows(block):
    return lax.all_gather(block, ("dp", "fsdp"), axis=0)


def scatter_rows(blocks):
    owned = lax.psum_scatter(blocks, ("dp", "fsdp"), scatter_dimension=0, tiled=True)
    return owned[0].astype(jnp.float32)


def shards(
    tokens,
    lengths,
    cotangent,
    query_weight,
    query_bias,
    key_weight,
    value_weight,
    value_bias,
    out_weight,
    out_bias,
    norm1_gain,
    norm1_shift,
    inner_weight,
    inner_bias,
    outer_weight,
    outer_bias,
    norm2_gain,
    norm2_shift,
):
    bf16 = jnp.bfloat16
    length = lengths[0]
    share = query_weight.shape[0]
    wide = FF // D
    devices = lax.axis_size("dp") * lax.axis_size("fsdp")
    used = (4 + 2 * wide) * share + 1
    rows = round_up(used, 16)
    packed = jnp.concatenate(
        [query_weight, key_weight, value_weight, out_weight]
        + [inner_weight[:, j * D : (j + 1) * D] for j in range(wide)]
        + [
            outer_weight,
            to_row(
                [
                    query_bias,
                    value_bias,
                    out_bias,
                    norm1_gain,
                    norm1_shift,
                    outer_bias,
                    norm2_gain,
                    norm2_shift,
                    inner_bias,
                ],
                bf16,
            ),
            jnp.zeros((rows - used, D), bf16),
        ],
        0,
    )
    every = gather_rows(packed)

    def matrix(start, count):
        return every[:, start * share : (start + count) * share].reshape(-1, D)

    small = every[:, used - 1]

    def vector(start, count=1):
        return small[:, start * share : (start + count) * share].reshape(-1)

    whole = (
        matrix(0, 1),
        vector(0),
        matrix(1, 1),
        matrix(2, 1),
        vector(1),
        matrix(3, 1),
        vector(2),
        vector(3),
        vector(4),
        jnp.concatenate([matrix(4 + j, 1) for j in range(wide)], 1),
        vector(8, wide),
        matrix(4 + wide, wide),
        vector(5),
        vector(6),
        vector(7),
    )
    layer_out, saved = forward_pass(tokens, length, whole)
    grad_tokens, sums, factors = backward_pass(tokens, cotangent, length, whole, saved)
    tok_rows, d_query, d_keys, d_values, mixed, d_first_b, hidden_b, d_pre_b, act_b, d_second_b = (
        factors
    )
    factor = 1.0 / jnp.sqrt(jnp.float32(tokens.shape[0] * devices))

    def weight_block(left, right):
        block = lax.dot_general(
            left, right, (((0,), (0,)), ((), ())), preferred_element_type=jnp.float32
        )
        return block.astype(bf16).reshape(devices, -1, D)

    split = [g.reshape(devices, -1) for g in sums]
    order = (0, 1, 2, 3, 4, 6, 7, 8, 5)
    terms = jnp.concatenate(
        [
            weight_block(tok_rows, d_query),
            weight_block(tok_rows, d_keys),
            weight_block(tok_rows, d_values),
            weight_block(mixed, d_first_b),
        ]
        + [weight_block(hidden_b, d_pre_b[:, j * D : (j + 1) * D]) for j in range(wide)]
        + [
            weight_block(act_b, d_second_b),
            to_row([split[i] for i in order], bf16),
            jnp.zeros((devices, rows - used, D), bf16),
        ],
        1,
    )
    owned = scatter_rows(terms) * factor

    def mine(start, count=1):
        return owned[start * share : (start + count) * share]

    def mine_small(start, count=1):
        return owned[used - 1, start * share : (start + count) * share]

    return (
        layer_out,
        grad_tokens,
        mine(0),
        mine_small(0),
        mine(1),
        mine(2),
        mine_small(1),
        mine(3),
        mine_small(2),
        mine_small(3),
        mine_small(4),
        jnp.concatenate([mine(4 + j) for j in range(wide)], 1),
        mine_small(8, wide),
        mine(4 + wide, wide),
        mine_small(5),
        mine_small(6),
        mine_small(7),
    )


def solution(mesh):
    placed = (
        P(("dp", "fsdp"), None),
        P(("dp", "fsdp")),
        P(("dp", "fsdp"), None),
        P(("dp", "fsdp"), None),
        P(("dp", "fsdp")),
        P(("dp", "fsdp"), None),
        P(("dp", "fsdp"), None),
        P(("dp", "fsdp")),
        P(("dp", "fsdp"), None),
        P(("dp", "fsdp")),
        P(("dp", "fsdp")),
        P(("dp", "fsdp")),
        P(("dp", "fsdp"), None),
        P(("dp", "fsdp")),
        P(("dp", "fsdp"), None),
        P(("dp", "fsdp")),
        P(("dp", "fsdp")),
        P(("dp", "fsdp")),
    )
    return jax.shard_map(
        shards,
        mesh=mesh,
        in_specs=placed,
        out_specs=(
            P(("dp", "fsdp"), None),
            P(("dp", "fsdp"), None),
            P(("dp", "fsdp"), None),
            P(("dp", "fsdp")),
            P(("dp", "fsdp"), None),
            P(("dp", "fsdp"), None),
            P(("dp", "fsdp")),
            P(("dp", "fsdp"), None),
            P(("dp", "fsdp")),
            P(("dp", "fsdp")),
            P(("dp", "fsdp")),
            P(("dp", "fsdp"), None),
            P(("dp", "fsdp")),
            P(("dp", "fsdp"), None),
            P(("dp", "fsdp")),
            P(("dp", "fsdp")),
            P(("dp", "fsdp")),
        ),
        check_vma=False,
    )
```

```python
import functools
import math

import jax
import jax.numpy as jnp
from jax import lax
from jax.experimental import pallas as pl
from jax.experimental.pallas import tpu as pltpu
from jax.sharding import PartitionSpec as P

D = 768
HEADS = 12
HEAD_DIM = 64
FF = 3072


NORM_EPS = 1e-12
ATTN_SCALE = 0.125


def layer_norm(summed, gain, shift):
    center = summed - jnp.mean(summed, -1, keepdims=True)
    rstd = lax.rsqrt(jnp.mean(center * center, -1, keepdims=True) + NORM_EPS)
    normed = center * rstd
    return (normed * gain.astype(jnp.float32) + shift.astype(jnp.float32), normed, rstd)


def norm_back(grad_in, normed, rstd, gain):
    scaled = grad_in * gain.astype(jnp.float32)
    return rstd * (
        scaled
        - jnp.mean(scaled, -1, keepdims=True)
        - normed * jnp.mean(scaled * normed, -1, keepdims=True)
    )


def gelu_parts(pre):
    cdf = 0.5 * (1.0 + jax.scipy.special.erf(pre * 0.7071067811865476))
    slope = cdf + pre * jnp.exp(-0.5 * pre * pre) * 0.3989422804014327
    return (pre * cdf, slope)


def heads_of(rows):
    return rows.reshape(rows.shape[0], HEADS, HEAD_DIM)


def get_scores(query, keys, length):
    scores = (
        jnp.einsum(
            "qhd,khd->hqk", heads_of(query), heads_of(keys), preferred_element_type=jnp.float32
        )
        * ATTN_SCALE
    )
    valid = jnp.arange(scores.shape[-1]) < length
    return jnp.where(valid[None, None, :], scores, -1e30)


def forward_pass(tokens, length, weights):
    (
        query_weight,
        query_bias,
        key_weight,
        value_weight,
        value_bias,
        out_weight,
        out_bias,
        norm1_gain,
        norm1_shift,
        inner_weight,
        inner_bias,
        outer_weight,
        outer_bias,
        norm2_gain,
        norm2_shift,
    ) = weights
    f32 = jnp.float32
    bf16 = jnp.bfloat16
    query = (
        jnp.dot(tokens, query_weight, preferred_element_type=f32) + query_bias.astype(f32)
    ).astype(bf16)
    keys = jnp.dot(tokens, key_weight, preferred_element_type=f32).astype(bf16)
    values = (
        jnp.dot(tokens, value_weight, preferred_element_type=f32) + value_bias.astype(f32)
    ).astype(bf16)
    scores = get_scores(query, keys, length)
    top = jnp.max(scores, -1)
    lse = top + jnp.log(jnp.sum(jnp.exp(scores - top[..., None]), -1))
    probs_b = jnp.exp(scores - lse[..., None]).astype(bf16)
    mixed = jnp.einsum("hqk,khd->qhd", probs_b, heads_of(values), preferred_element_type=f32)
    mixed = mixed.reshape(tokens.shape[0], -1).astype(bf16)
    first_sum = (
        tokens.astype(f32)
        + jnp.dot(mixed, out_weight, preferred_element_type=f32)
        + out_bias.astype(f32)
    )
    hidden, normed_one, rstd_one = layer_norm(first_sum, norm1_gain, norm1_shift)
    hidden_b = hidden.astype(bf16)
    pre = jnp.dot(hidden_b, inner_weight, preferred_element_type=f32) + inner_bias.astype(f32)
    act, slope = gelu_parts(pre)
    act_b = act.astype(bf16)
    second_sum = (
        hidden + jnp.dot(act_b, outer_weight, preferred_element_type=f32) + outer_bias.astype(f32)
    )
    layer_out, normed_two, rstd_two = layer_norm(second_sum, norm2_gain, norm2_shift)
    saved = (
        query,
        keys,
        values,
        lse,
        mixed,
        normed_one,
        rstd_one,
        hidden_b,
        slope,
        act_b,
        normed_two,
        rstd_two,
    )
    return (layer_out, saved)


def backward_pass(tokens, cotangent, length, weights, saved):
    (
        query_weight,
        query_bias,
        key_weight,
        value_weight,
        value_bias,
        out_weight,
        out_bias,
        norm1_gain,
        norm1_shift,
        inner_weight,
        inner_bias,
        outer_weight,
        outer_bias,
        norm2_gain,
        norm2_shift,
    ) = weights
    (
        query,
        keys,
        values,
        lse,
        mixed,
        normed_one,
        rstd_one,
        hidden_b,
        slope,
        act_b,
        normed_two,
        rstd_two,
    ) = saved
    f32 = jnp.float32
    bf16 = jnp.bfloat16
    d_second = norm_back(cotangent, normed_two, rstd_two, norm2_gain)
    d_second_b = d_second.astype(bf16)
    d_pre = jnp.dot(d_second_b, outer_weight.T, preferred_element_type=f32) * slope
    d_pre_b = d_pre.astype(bf16)
    d_hidden = d_second + jnp.dot(d_pre_b, inner_weight.T, preferred_element_type=f32)
    d_first = norm_back(d_hidden, normed_one, rstd_one, norm1_gain)
    d_first_b = d_first.astype(bf16)
    d_mixed = jnp.dot(d_first_b, out_weight.T, preferred_element_type=f32).astype(bf16)
    again = jnp.exp(get_scores(query, keys, length) - lse[..., None])
    again_b = again.astype(bf16)
    d_probs = jnp.einsum(
        "qhd,khd->hqk", heads_of(d_mixed), heads_of(values), preferred_element_type=f32
    )
    d_values_f = jnp.einsum(
        "hqk,qhd->khd", again_b, heads_of(d_mixed), preferred_element_type=f32
    ).reshape(tokens.shape[0], -1)
    delta = jnp.sum(again * d_probs, -1, keepdims=True)
    d_scores = (again * (d_probs - delta) * ATTN_SCALE).astype(bf16)
    d_query_f = jnp.einsum(
        "hqk,khd->qhd", d_scores, heads_of(keys), preferred_element_type=f32
    ).reshape(tokens.shape[0], -1)
    d_keys_f = jnp.einsum(
        "hqk,qhd->khd", d_scores, heads_of(query), preferred_element_type=f32
    ).reshape(tokens.shape[0], -1)
    d_query = d_query_f.astype(bf16)
    d_keys = d_keys_f.astype(bf16)
    d_values = d_values_f.astype(bf16)
    grad_tokens = (
        d_first
        + jnp.dot(d_query, query_weight.T, preferred_element_type=f32)
        + jnp.dot(d_keys, key_weight.T, preferred_element_type=f32)
        + jnp.dot(d_values, value_weight.T, preferred_element_type=f32)
    )
    small = (
        jnp.sum(d_query_f, 0),
        jnp.sum(d_values_f, 0),
        jnp.sum(d_first, 0),
        jnp.sum(d_hidden * normed_one, 0),
        jnp.sum(d_hidden, 0),
        jnp.sum(d_pre, 0),
        jnp.sum(d_second, 0),
        jnp.sum(cotangent * normed_two, 0),
        jnp.sum(cotangent, 0),
    )
    factors = (
        tokens,
        d_query,
        d_keys,
        d_values,
        mixed,
        d_first_b,
        hidden_b,
        d_pre_b,
        act_b,
        d_second_b,
    )
    return (grad_tokens, small, factors)


MESH = pl.DeviceIdType.MESH
LANES = 128


class Place:
    def __init__(self, side, depth):
        self.side, self.depth = side, depth
        dp, fsdp = lax.axis_index("dp"), lax.axis_index("fsdp")
        self.c = fsdp % 2
        self.z = fsdp // 2
        row, col = dp // side, dp % side
        self.a = (1 - self.c) * col + self.c * row
        self.b = (1 - self.c) * row + self.c * col
        self.dp = dp

    def column(self, a, b, c):
        return (1 - c) * (b * self.side + a) + c * (a * self.side + b)

    def device(self, da=0, db=0, dz=0):
        a, b = (self.a + da) % self.side, (self.b + db) % self.side
        z = (self.z + dz) % self.depth
        return (self.column(a, b, self.c), z * 2 + self.c)

    def block(self, da, db, dz):
        dp, fsdp = self.device(da, db, dz)
        return dp * (2 * self.depth) + fsdp

    def sibling(self):
        return (self.dp, self.z * 2 + 1 - self.c)

    def sibling_block(self, da, db, dz):
        c = 1 - self.c
        a, b = (self.b + da) % self.side, (self.a + db) % self.side
        z = (self.z + dz) % self.depth
        return self.column(a, b, c) * (2 * self.depth) + z * 2 + c


def meet(place):
    barrier = pltpu.get_barrier_semaphore()
    others = [place.device(da=k) for k in range(1, place.side)]
    others += [place.device(db=k) for k in range(1, place.side)]
    others += [place.device(dz=k) for k in range(1, place.depth)]
    others.append(place.sibling())
    for other in others:
        pl.semaphore_signal(barrier, inc=1, device_id=other, device_id_type=MESH)
    pl.semaphore_wait(barrier, len(others))


def gather_kernel(side, depth, a_ref, b_ref, a_out, b_out, keep, sent, got):
    place = Place(side, depth)
    meet(place)
    pairs = ((a_ref, a_out), (b_ref, b_out))
    me = place.block(0, 0, 0)
    own = [
        pltpu.make_async_copy(src.at[0], dst.at[me], keep.at[i])
        for i, (src, dst) in enumerate(pairs)
    ]
    for copy in own:
        copy.start()
    started = []
    half = side * side * depth

    def slot(da, db, dz):
        return (db * side + da) * depth + dz

    def push(source, device, at, index, sem_at):
        for i, (src, dst) in enumerate(pairs):
            origin = src.at[0] if source is None else dst.at[source]
            copy = pltpu.make_async_remote_copy(
                src_ref=origin,
                dst_ref=dst.at[at],
                send_sem=sent.at[i, len(started) // 2],
                recv_sem=got.at[i, sem_at],
                device_id=device,
                device_id_type=MESH,
            )
            copy.start()
            started.append(copy)

    def landed(index, sem_at):
        for i, (src, dst) in enumerate(pairs):
            pltpu.make_async_copy(dst.at[index], dst.at[index], got.at[i, sem_at]).wait()

    def spread(source, da, db, dz):
        index = place.block(da, db, dz)
        if da == 0 and db == 0:
            for k in range(1, side):
                push(source, place.device(da=k), index, index, slot((side - k) % side, 0, dz))
        if db == 0:
            for k in range(1, side):
                push(source, place.device(db=k), index, index, slot(da, (side - k) % side, dz))
        push(source, place.sibling(), index, index, half + slot(da, db, dz))

    for dz in range(1, depth):
        push(None, place.device(dz=dz), me, me, slot(0, 0, depth - dz))
    spread(None, 0, 0, 0)
    near = sorted(range(1, depth), key=lambda k: min(k, depth - k))
    steps = []
    for rank, dz in enumerate([0] + near):
        for db in range(side):
            for da in range(side):
                if (da, db, dz) != (0, 0, 0):
                    steps.append((rank + (da > 0) + 2 * (db > 0), da, db, dz))
    for _, da, db, dz in sorted(steps):
        index = place.block(da, db, dz)
        landed(index, slot(da, db, dz))
        spread(index, da, db, dz)
    for db in range(side):
        for da in range(side):
            for dz in range(depth):
                landed(place.sibling_block(da, db, dz), half + slot(da, db, dz))
    for copy in own:
        copy.wait()
    for copy in started:
        copy.wait_send()


def kernels_fit():
    side = math.isqrt(lax.axis_size("dp"))
    devices = lax.axis_size("dp") * lax.axis_size("fsdp")
    return side * side == lax.axis_size("dp") and lax.axis_size("fsdp") % 2 == 0 and devices <= 32


def gather_blocks(a_block, b_block):
    if not kernels_fit():
        return tuple(lax.all_gather(v, ("dp", "fsdp"), axis=0) for v in (a_block, b_block))
    side, depth = math.isqrt(lax.axis_size("dp")), lax.axis_size("fsdp") // 2
    devices = 2 * side * side * depth
    anywhere = pl.BlockSpec(memory_space=pl.ANY)
    return pl.pallas_call(
        functools.partial(gather_kernel, side, depth),
        name="gather_blocks",
        out_shape=tuple(
            jax.ShapeDtypeStruct((devices,) + v.shape, v.dtype) for v in (a_block, b_block)
        ),
        in_specs=[anywhere] * 2,
        out_specs=(anywhere,) * 2,
        scratch_shapes=[
            pltpu.SemaphoreType.DMA((2,)),
            pltpu.SemaphoreType.DMA((2, devices)),
            pltpu.SemaphoreType.DMA((2, devices)),
        ],
        compiler_params=pltpu.CompilerParams(collective_id=0, has_side_effects=True),
    )(a_block[None], b_block[None])


def scatter_kernel(side, depth, a_in, b_in, a_out, b_out, *scratch):
    a_bufs, b_bufs = scratch[0:4], scratch[4:8]
    sent, got = scratch[8:10]
    place = Place(side, depth)
    meet(place)
    started = []
    half = side * side * depth
    first2 = half
    first3 = first2 + (side - 1) * side * depth
    first4 = first3 + (side - 1) * depth
    groups = ((a_in, a_bufs, a_out), (b_in, b_bufs, b_out))

    def slot(da, db, dz):
        return (db * side + da) * depth + dz

    def push(pick_source, level, at, device, sem_at):
        for i, (data, bufs, _) in enumerate(groups):
            copy = pltpu.make_async_remote_copy(
                src_ref=pick_source(data, bufs),
                dst_ref=bufs[level].at[at],
                send_sem=sent.at[i, len(started) // 2],
                recv_sem=got.at[i, sem_at],
                device_id=device,
                device_id_type=MESH,
            )
            copy.start()
            started.append(copy)

    def landed(level, at, sem_at):
        for i, (_, bufs, _) in enumerate(groups):
            ref = bufs[level].at[at]
            pltpu.make_async_copy(ref, ref, got.at[i, sem_at]).wait()

    def add(k, block, extra, final=False):
        for data, bufs, out in groups:
            rows, lanes = data.shape[1:]
            wide = lanes > D
            step = lanes // 7 if wide else rows // 6
            count = 7 if wide else 6

            def body(n, _):
                if wide:
                    at = (slice(None), pl.ds(pl.multiple_of(n * step, LANES), step))
                else:
                    at = (pl.ds(pl.multiple_of(n * step, 16), step), slice(None))
                total = bufs[0][(k,) + at].astype(jnp.float32)
                total += data[(block,) + at].astype(jnp.float32)
                for level, e in extra:
                    total += bufs[level][(e,) + at].astype(jnp.float32)
                if final:
                    out[at] = total
                else:
                    bufs[0][(k,) + at] = total.astype(jnp.bfloat16)
                return 0

            lax.fori_loop(0, count, body, 0)

    order = [
        (da, db, dz)
        for db in range(side - 1, -1, -1)
        for da in range(side - 1, -1, -1)
        for dz in range(depth - 1, -1, -1)
    ]
    for da, db, dz in order:
        index = place.sibling_block(da, db, dz)
        k = slot(da, db, dz)
        push(lambda data, bufs: data.at[index], 0, k, place.sibling(), k)
    for da, db, dz in order:
        k = slot(da, db, dz)
        landed(0, k, k)
        extra = []
        if db == 0:
            for d in range(1, side):
                e = (d - 1) * side * depth + da * depth + dz
                landed(1, e, first2 + e)
                extra.append((1, e))
        if db == 0 and da == 0:
            for d in range(1, side):
                e = (d - 1) * depth + dz
                landed(2, e, first3 + e)
                extra.append((2, e))
        if (da, db, dz) == (0, 0, 0):
            for d in range(1, depth):
                landed(3, d - 1, first4 + d - 1)
                extra.append((3, d - 1))
        add(k, place.block(da, db, dz), extra, final=(da, db, dz) == (0, 0, 0))
        source = lambda data, bufs: bufs[0].at[k]
        if db:
            e = (db - 1) * side * depth + da * depth + dz
            push(source, 1, e, place.device(db=db), first2 + e)
        elif da:
            e = (da - 1) * depth + dz
            push(source, 2, e, place.device(da=da), first3 + e)
        elif dz:
            push(source, 3, dz - 1, place.device(dz=dz), first4 + dz - 1)
    for copy in started:
        copy.wait_send()


def scatter_blocks(a_terms, b_terms):
    if not kernels_fit():
        return tuple(
            lax.psum_scatter(v, ("dp", "fsdp"), scatter_dimension=0, tiled=True)[0].astype(
                jnp.float32
            )
            for v in (a_terms, b_terms)
        )
    side, depth = math.isqrt(lax.axis_size("dp")), lax.axis_size("fsdp") // 2
    half = side * side * depth
    counts = (half, (side - 1) * side * depth, (side - 1) * depth, depth - 1)
    vmem = pl.BlockSpec(memory_space=pltpu.VMEM)
    return pl.pallas_call(
        functools.partial(scatter_kernel, side, depth),
        name="scatter_blocks",
        out_shape=tuple(
            jax.ShapeDtypeStruct(v.shape[1:], jnp.float32) for v in (a_terms, b_terms)
        ),
        in_specs=[vmem] * 2,
        out_specs=(vmem,) * 2,
        scratch_shapes=[
            pltpu.VMEM((max(n, 1),) + v.shape[1:], v.dtype)
            for v in (a_terms, b_terms)
            for n in counts
        ]
        + [pltpu.SemaphoreType.DMA((2, 2 * half)), pltpu.SemaphoreType.DMA((2, 2 * half))],
        compiler_params=pltpu.CompilerParams(
            collective_id=1, has_side_effects=True, vmem_limit_bytes=52 * 2**20
        ),
    )(a_terms, b_terms)


def shards(
    tokens,
    lengths,
    cotangent,
    query_weight,
    query_bias,
    key_weight,
    value_weight,
    value_bias,
    out_weight,
    out_bias,
    norm1_gain,
    norm1_shift,
    inner_weight,
    inner_bias,
    outer_weight,
    outer_bias,
    norm2_gain,
    norm2_shift,
):
    bf16 = jnp.bfloat16
    length = lengths[0]
    share = query_weight.shape[0]
    wide = FF // D
    devices = lax.axis_size("dp") * lax.axis_size("fsdp")
    start = 4 * D + FF

    def columns(vectors):
        side_by_side = jnp.concatenate([v.reshape(-1, n) for v, n in vectors], 1).astype(bf16)
        return jnp.pad(side_by_side, ((0, 0), (0, LANES - side_by_side.shape[1])))

    packed = jnp.concatenate(
        [
            query_weight,
            key_weight,
            value_weight,
            out_weight,
            inner_weight,
            columns(
                [
                    (query_bias, 1),
                    (value_bias, 1),
                    (out_bias, 1),
                    (norm1_gain, 1),
                    (norm1_shift, 1),
                    (outer_bias, 1),
                    (norm2_gain, 1),
                    (norm2_shift, 1),
                    (inner_bias, wide),
                ]
            ),
        ],
        1,
    )
    every, outer = gather_blocks(packed, outer_weight)
    every = every.reshape(-1, every.shape[-1])
    vectors = every[:, start:].T

    whole = (
        every[:, 0:D],
        vectors[0],
        every[:, D : 2 * D],
        every[:, 2 * D : 3 * D],
        vectors[1],
        every[:, 3 * D : 4 * D],
        vectors[2],
        vectors[3],
        vectors[4],
        every[:, 4 * D : start],
        vectors[8 : 8 + wide].T.reshape(-1),
        outer.reshape(FF, D),
        vectors[5],
        vectors[6],
        vectors[7],
    )
    layer_out, saved = forward_pass(tokens, length, whole)
    grad_tokens, sums, factors = backward_pass(tokens, cotangent, length, whole, saved)
    tok_rows, d_query, d_keys, d_values, mixed, d_first_b, hidden_b, d_pre_b, act_b, d_second_b = (
        factors
    )
    factor = 1.0 / jnp.sqrt(jnp.float32(tokens.shape[0] * devices))

    def weight_block(left, right):
        return lax.dot_general(
            left, right, (((0,), (0,)), ((), ())), preferred_element_type=jnp.float32
        ).astype(bf16)

    order = (0, 1, 2, 3, 4, 6, 7, 8, 5)
    terms = jnp.concatenate(
        [
            weight_block(tok_rows, d_query),
            weight_block(tok_rows, d_keys),
            weight_block(tok_rows, d_values),
            weight_block(mixed, d_first_b),
            weight_block(hidden_b, d_pre_b),
            columns([(sums[i], wide if i == 5 else 1) for i in order]),
        ],
        1,
    )
    owned, owned_outer = scatter_blocks(
        terms.reshape(devices, share, -1), weight_block(act_b, d_second_b).reshape(devices, -1, D)
    )
    owned = owned * factor
    owned_vectors = owned[:, start:].T

    return (
        layer_out,
        grad_tokens,
        owned[:, 0:D],
        owned_vectors[0],
        owned[:, D : 2 * D],
        owned[:, 2 * D : 3 * D],
        owned_vectors[1],
        owned[:, 3 * D : 4 * D],
        owned_vectors[2],
        owned_vectors[3],
        owned_vectors[4],
        owned[:, 4 * D : start],
        owned_vectors[8 : 8 + wide].T.reshape(-1),
        owned_outer * factor,
        owned_vectors[5],
        owned_vectors[6],
        owned_vectors[7],
    )


def solution(mesh):
    placed = (
        P(("dp", "fsdp"), None),
        P(("dp", "fsdp")),
        P(("dp", "fsdp"), None),
        P(("dp", "fsdp"), None),
        P(("dp", "fsdp")),
        P(("dp", "fsdp"), None),
        P(("dp", "fsdp"), None),
        P(("dp", "fsdp")),
        P(("dp", "fsdp"), None),
        P(("dp", "fsdp")),
        P(("dp", "fsdp")),
        P(("dp", "fsdp")),
        P(("dp", "fsdp"), None),
        P(("dp", "fsdp")),
        P(("dp", "fsdp"), None),
        P(("dp", "fsdp")),
        P(("dp", "fsdp")),
        P(("dp", "fsdp")),
    )
    return jax.shard_map(
        shards,
        mesh=mesh,
        in_specs=placed,
        out_specs=(
            P(("dp", "fsdp"), None),
            P(("dp", "fsdp"), None),
            P(("dp", "fsdp"), None),
            P(("dp", "fsdp")),
            P(("dp", "fsdp"), None),
            P(("dp", "fsdp"), None),
            P(("dp", "fsdp")),
            P(("dp", "fsdp"), None),
            P(("dp", "fsdp")),
            P(("dp", "fsdp")),
            P(("dp", "fsdp")),
            P(("dp", "fsdp"), None),
            P(("dp", "fsdp")),
            P(("dp", "fsdp"), None),
            P(("dp", "fsdp")),
            P(("dp", "fsdp")),
            P(("dp", "fsdp")),
        ),
        check_vma=False,
    )
```

```python
import functools
import math

import jax
import jax.numpy as jnp
from jax import lax
from jax.experimental import pallas as pl
from jax.experimental.pallas import tpu as pltpu
from jax.sharding import PartitionSpec as P

D = 768
HEADS = 12
HEAD_DIM = 64
FF = 3072


NORM_EPS = 1e-12
ATTN_SCALE = 0.125


def layer_norm(summed, gain, shift):
    center = summed - jnp.mean(summed, -1, keepdims=True)
    rstd = lax.rsqrt(jnp.mean(center * center, -1, keepdims=True) + NORM_EPS)
    normed = center * rstd
    return (normed * gain.astype(jnp.float32) + shift.astype(jnp.float32), normed, rstd)


def norm_back(grad_in, normed, rstd, gain):
    scaled = grad_in * gain.astype(jnp.float32)
    return rstd * (
        scaled
        - jnp.mean(scaled, -1, keepdims=True)
        - normed * jnp.mean(scaled * normed, -1, keepdims=True)
    )


def gelu_parts(pre):
    cdf = 0.5 * (1.0 + jax.scipy.special.erf(pre * 0.7071067811865476))
    slope = cdf + pre * jnp.exp(-0.5 * pre * pre) * 0.3989422804014327
    return (pre * cdf, slope)


def heads_of(rows):
    return rows.reshape(rows.shape[0], HEADS, HEAD_DIM)


def get_scores(query, keys, length):
    scores = (
        jnp.einsum(
            "qhd,khd->hqk", heads_of(query), heads_of(keys), preferred_element_type=jnp.float32
        )
        * ATTN_SCALE
    )
    valid = jnp.arange(scores.shape[-1]) < length
    return jnp.where(valid[None, None, :], scores, -1e30)


def forward_pass(tokens, length, weights):
    (
        query_weight,
        query_bias,
        key_weight,
        value_weight,
        value_bias,
        out_weight,
        out_bias,
        norm1_gain,
        norm1_shift,
        inner_weight,
        inner_bias,
        outer_weight,
        outer_bias,
        norm2_gain,
        norm2_shift,
    ) = weights
    f32 = jnp.float32
    bf16 = jnp.bfloat16
    query = (
        jnp.dot(tokens, query_weight, preferred_element_type=f32) + query_bias.astype(f32)
    ).astype(bf16)
    keys = jnp.dot(tokens, key_weight, preferred_element_type=f32).astype(bf16)
    values = (
        jnp.dot(tokens, value_weight, preferred_element_type=f32) + value_bias.astype(f32)
    ).astype(bf16)
    scores = get_scores(query, keys, length)
    top = jnp.max(scores, -1)
    lse = top + jnp.log(jnp.sum(jnp.exp(scores - top[..., None]), -1))
    probs_b = jnp.exp(scores - lse[..., None]).astype(bf16)
    mixed = jnp.einsum("hqk,khd->qhd", probs_b, heads_of(values), preferred_element_type=f32)
    mixed = mixed.reshape(tokens.shape[0], -1).astype(bf16)
    first_sum = (
        tokens.astype(f32)
        + jnp.dot(mixed, out_weight, preferred_element_type=f32)
        + out_bias.astype(f32)
    )
    hidden, normed_one, rstd_one = layer_norm(first_sum, norm1_gain, norm1_shift)
    hidden_b = hidden.astype(bf16)
    pre = jnp.dot(hidden_b, inner_weight, preferred_element_type=f32) + inner_bias.astype(f32)
    act, slope = gelu_parts(pre)
    act_b = act.astype(bf16)
    second_sum = (
        hidden + jnp.dot(act_b, outer_weight, preferred_element_type=f32) + outer_bias.astype(f32)
    )
    layer_out, normed_two, rstd_two = layer_norm(second_sum, norm2_gain, norm2_shift)
    saved = (
        query,
        keys,
        values,
        lse,
        mixed,
        normed_one,
        rstd_one,
        hidden_b,
        slope,
        act_b,
        normed_two,
        rstd_two,
    )
    return (layer_out, saved)


def backward_pass(tokens, cotangent, length, weights, saved):
    (
        query_weight,
        query_bias,
        key_weight,
        value_weight,
        value_bias,
        out_weight,
        out_bias,
        norm1_gain,
        norm1_shift,
        inner_weight,
        inner_bias,
        outer_weight,
        outer_bias,
        norm2_gain,
        norm2_shift,
    ) = weights
    (
        query,
        keys,
        values,
        lse,
        mixed,
        normed_one,
        rstd_one,
        hidden_b,
        slope,
        act_b,
        normed_two,
        rstd_two,
    ) = saved
    f32 = jnp.float32
    bf16 = jnp.bfloat16
    d_second = norm_back(cotangent, normed_two, rstd_two, norm2_gain)
    d_second_b = d_second.astype(bf16)
    d_pre = jnp.dot(d_second_b, outer_weight.T, preferred_element_type=f32) * slope
    d_pre_b = d_pre.astype(bf16)
    d_hidden = d_second + jnp.dot(d_pre_b, inner_weight.T, preferred_element_type=f32)
    d_first = norm_back(d_hidden, normed_one, rstd_one, norm1_gain)
    d_first_b = d_first.astype(bf16)
    d_mixed = jnp.dot(d_first_b, out_weight.T, preferred_element_type=f32).astype(bf16)
    again = jnp.exp(get_scores(query, keys, length) - lse[..., None])
    again_b = again.astype(bf16)
    d_probs = jnp.einsum(
        "qhd,khd->hqk", heads_of(d_mixed), heads_of(values), preferred_element_type=f32
    )
    d_values_f = jnp.einsum(
        "hqk,qhd->khd", again_b, heads_of(d_mixed), preferred_element_type=f32
    ).reshape(tokens.shape[0], -1)
    delta = jnp.sum(again * d_probs, -1, keepdims=True)
    d_scores = (again * (d_probs - delta) * ATTN_SCALE).astype(bf16)
    d_query_f = jnp.einsum(
        "hqk,khd->qhd", d_scores, heads_of(keys), preferred_element_type=f32
    ).reshape(tokens.shape[0], -1)
    d_keys_f = jnp.einsum(
        "hqk,qhd->khd", d_scores, heads_of(query), preferred_element_type=f32
    ).reshape(tokens.shape[0], -1)
    d_query = d_query_f.astype(bf16)
    d_keys = d_keys_f.astype(bf16)
    d_values = d_values_f.astype(bf16)
    grad_tokens = (
        d_first
        + jnp.dot(d_query, query_weight.T, preferred_element_type=f32)
        + jnp.dot(d_keys, key_weight.T, preferred_element_type=f32)
        + jnp.dot(d_values, value_weight.T, preferred_element_type=f32)
    )
    small = (
        jnp.sum(d_query_f, 0),
        jnp.sum(d_values_f, 0),
        jnp.sum(d_first, 0),
        jnp.sum(d_hidden * normed_one, 0),
        jnp.sum(d_hidden, 0),
        jnp.sum(d_pre, 0),
        jnp.sum(d_second, 0),
        jnp.sum(cotangent * normed_two, 0),
        jnp.sum(cotangent, 0),
    )
    factors = (
        tokens,
        d_query,
        d_keys,
        d_values,
        mixed,
        d_first_b,
        hidden_b,
        d_pre_b,
        act_b,
        d_second_b,
    )
    return (grad_tokens, small, factors)


MESH = pl.DeviceIdType.MESH
LANES = 128


class Place:
    def __init__(self, side, depth):
        self.side, self.depth = side, depth
        dp, fsdp = lax.axis_index("dp"), lax.axis_index("fsdp")
        self.c = fsdp % 2
        self.z = fsdp // 2
        row, col = dp // side, dp % side
        self.a = (1 - self.c) * col + self.c * row
        self.b = (1 - self.c) * row + self.c * col
        self.dp = dp

    def column(self, a, b, c):
        return (1 - c) * (b * self.side + a) + c * (a * self.side + b)

    def device(self, da=0, db=0, dz=0):
        a, b = (self.a + da) % self.side, (self.b + db) % self.side
        z = (self.z + dz) % self.depth
        return (self.column(a, b, self.c), z * 2 + self.c)

    def block(self, da, db, dz):
        dp, fsdp = self.device(da, db, dz)
        return dp * (2 * self.depth) + fsdp

    def sibling(self):
        return (self.dp, self.z * 2 + 1 - self.c)

    def sibling_block(self, da, db, dz):
        c = 1 - self.c
        a, b = (self.b + da) % self.side, (self.a + db) % self.side
        z = (self.z + dz) % self.depth
        return self.column(a, b, c) * (2 * self.depth) + z * 2 + c


def greet(place):
    barrier = pltpu.get_barrier_semaphore()
    others = [place.device(da=k) for k in range(1, place.side)]
    others += [place.device(db=k) for k in range(1, place.side)]
    others += [place.device(dz=k) for k in range(1, place.depth)]
    others.append(place.sibling())
    for other in others:
        pl.semaphore_signal(barrier, inc=1, device_id=other, device_id_type=MESH)
    return len(others)


def gather_kernel(side, depth, parts, *refs):
    part_refs = refs[:parts]
    b_ref, a_out, b_out, a_ref, keep, sent, got = refs[parts:]
    place = Place(side, depth)
    greeted = greet(place)
    at = 0
    for part in part_refs:
        a_ref[0, :, at : at + part.shape[1]] = part[...]
        at += part.shape[1]
    pl.semaphore_wait(pltpu.get_barrier_semaphore(), greeted)
    pairs = ((a_ref, a_out), (b_ref, b_out))
    me = place.block(0, 0, 0)
    own = [
        pltpu.make_async_copy(src.at[0], dst.at[me], keep.at[i])
        for i, (src, dst) in enumerate(pairs)
    ]
    for copy in own:
        copy.start()
    started = []
    half = side * side * depth

    def slot(da, db, dz):
        return (db * side + da) * depth + dz

    def push(source, device, at, index, sem_at):
        for i, (src, dst) in enumerate(pairs):
            origin = src.at[0] if source is None else dst.at[source]
            copy = pltpu.make_async_remote_copy(
                src_ref=origin,
                dst_ref=dst.at[at],
                send_sem=sent.at[i, len(started) // 2],
                recv_sem=got.at[i, sem_at],
                device_id=device,
                device_id_type=MESH,
            )
            copy.start()
            started.append(copy)

    def landed(index, sem_at):
        for i, (src, dst) in enumerate(pairs):
            pltpu.make_async_copy(dst.at[index], dst.at[index], got.at[i, sem_at]).wait()

    def spread(source, da, db, dz):
        index = place.block(da, db, dz)
        if da == 0 and db == 0:
            for k in range(1, side):
                push(source, place.device(da=k), index, index, slot((side - k) % side, 0, dz))
        if db == 0:
            for k in range(1, side):
                push(source, place.device(db=k), index, index, slot(da, (side - k) % side, dz))
        push(source, place.sibling(), index, index, half + slot(da, db, dz))

    for dz in range(1, depth):
        push(None, place.device(dz=dz), me, me, slot(0, 0, depth - dz))
    spread(None, 0, 0, 0)
    near = sorted(range(1, depth), key=lambda k: min(k, depth - k))
    steps = []
    for rank, dz in enumerate([0] + near):
        for db in range(side):
            for da in range(side):
                if (da, db, dz) != (0, 0, 0):
                    steps.append((rank + (da > 0) + 2 * (db > 0), da, db, dz))
    for _, da, db, dz in sorted(steps):
        index = place.block(da, db, dz)
        landed(index, slot(da, db, dz))
        spread(index, da, db, dz)
    for db in range(side):
        for da in range(side):
            for dz in range(depth):
                landed(place.sibling_block(da, db, dz), half + slot(da, db, dz))
    for copy in own:
        copy.wait()
    for copy in started:
        copy.wait_send()


def kernels_fit():
    side = math.isqrt(lax.axis_size("dp"))
    devices = lax.axis_size("dp") * lax.axis_size("fsdp")
    return side * side == lax.axis_size("dp") and lax.axis_size("fsdp") % 2 == 0 and devices <= 32


def gather_blocks(a_parts, b_block):
    if not kernels_fit():
        a_block = jnp.concatenate(a_parts, 1)
        return tuple(lax.all_gather(v, ("dp", "fsdp"), axis=0) for v in (a_block, b_block))
    side, depth = math.isqrt(lax.axis_size("dp")), lax.axis_size("fsdp") // 2
    devices = 2 * side * side * depth
    rows, lanes = b_block.shape[0], sum(v.shape[1] for v in a_parts)
    share = a_parts[0].shape[0]
    dtype = b_block.dtype
    anywhere = pl.BlockSpec(memory_space=pl.ANY)
    vmem = pl.BlockSpec(memory_space=pltpu.VMEM)
    return pl.pallas_call(
        functools.partial(gather_kernel, side, depth, len(a_parts)),
        name="gather_blocks",
        out_shape=(
            jax.ShapeDtypeStruct((devices, share, lanes), dtype),
            jax.ShapeDtypeStruct((devices, rows, D), dtype),
        ),
        in_specs=[vmem] * len(a_parts) + [anywhere],
        out_specs=(anywhere,) * 2,
        scratch_shapes=[
            pltpu.VMEM((1, share, lanes), dtype),
            pltpu.SemaphoreType.DMA((2,)),
            pltpu.SemaphoreType.DMA((2, devices)),
            pltpu.SemaphoreType.DMA((2, devices)),
        ],
        compiler_params=pltpu.CompilerParams(collective_id=0, has_side_effects=True),
    )(*a_parts, b_block[None])


def product(left, right):
    return lax.dot_general(
        left, right, (((0,), (0,)), ((), ())), preferred_element_type=jnp.float32
    )


def fill(factors, column_ref, a_in, b_in):
    tok, d_query, d_keys, d_values, mixed, d_first, hidden, d_pre, act, d_second = factors
    share, outer_share = a_in.shape[1], b_in.shape[1]
    part = D // 2
    pairs = [(tok, d_query, 0), (tok, d_keys, 0), (tok, d_values, 0), (mixed, d_first, 0)]
    pairs += [(hidden, d_pre, j * D) for j in range(FF // D)]
    for at, (left, right, lane) in enumerate(pairs):
        for m in range(0, D, part):
            block = product(left[:, m : m + part], right[:, lane : lane + D])
            block = block.reshape(part // share, share, D).astype(jnp.bfloat16)
            a_in[m // share : (m + part) // share, :, at * D : (at + 1) * D] = block
    a_in[:, :, len(pairs) * D :] = column_ref[...]
    for m in range(0, FF, part):
        block = product(act[:, m : m + part], d_second[...])
        block = block.reshape(part // outer_share, outer_share, D).astype(jnp.bfloat16)
        b_in[m // outer_share : (m + part) // outer_share] = block


def scatter_kernel(side, depth, *refs):
    factors, column_ref, a_out, b_out = refs[0:10], refs[10], refs[11], refs[12]
    a_in, b_in = refs[13:15]
    a_bufs, b_bufs = refs[15:19], refs[19:23]
    sent, got = refs[23:25]
    place = Place(side, depth)
    greeted = greet(place)
    fill(factors, column_ref, a_in, b_in)
    pl.semaphore_wait(pltpu.get_barrier_semaphore(), greeted)
    started = []
    half = side * side * depth
    first2 = half
    first3 = first2 + (side - 1) * side * depth
    first4 = first3 + (side - 1) * depth
    groups = ((a_in, a_bufs, a_out), (b_in, b_bufs, b_out))

    def slot(da, db, dz):
        return (db * side + da) * depth + dz

    def push(pick_source, level, at, device, sem_at):
        for i, (data, bufs, _) in enumerate(groups):
            copy = pltpu.make_async_remote_copy(
                src_ref=pick_source(data, bufs),
                dst_ref=bufs[level].at[at],
                send_sem=sent.at[i, len(started) // 2],
                recv_sem=got.at[i, sem_at],
                device_id=device,
                device_id_type=MESH,
            )
            copy.start()
            started.append(copy)

    def landed(level, at, sem_at):
        for i, (_, bufs, _) in enumerate(groups):
            ref = bufs[level].at[at]
            pltpu.make_async_copy(ref, ref, got.at[i, sem_at]).wait()

    def add(k, block, extra, final=False):
        for data, bufs, out in groups:
            rows, lanes = data.shape[1:]
            wide = lanes > D
            step = lanes // 7 if wide else rows // 6
            count = 7 if wide else 6

            def body(n, _):
                if wide:
                    at = (slice(None), pl.ds(pl.multiple_of(n * step, LANES), step))
                else:
                    at = (pl.ds(pl.multiple_of(n * step, 16), step), slice(None))
                total = bufs[0][(k,) + at].astype(jnp.float32)
                total += data[(block,) + at].astype(jnp.float32)
                for level, e in extra:
                    total += bufs[level][(e,) + at].astype(jnp.float32)
                if final:
                    out[at] = total
                else:
                    bufs[0][(k,) + at] = total.astype(jnp.bfloat16)
                return 0

            lax.fori_loop(0, count, body, 0)

    order = [
        (da, db, dz)
        for db in range(side - 1, -1, -1)
        for da in range(side - 1, -1, -1)
        for dz in range(depth - 1, -1, -1)
    ]
    for da, db, dz in order:
        index = place.sibling_block(da, db, dz)
        k = slot(da, db, dz)
        push(lambda data, bufs: data.at[index], 0, k, place.sibling(), k)
    for da, db, dz in order:
        k = slot(da, db, dz)
        landed(0, k, k)
        extra = []
        if db == 0:
            for d in range(1, side):
                e = (d - 1) * side * depth + da * depth + dz
                landed(1, e, first2 + e)
                extra.append((1, e))
        if db == 0 and da == 0:
            for d in range(1, side):
                e = (d - 1) * depth + dz
                landed(2, e, first3 + e)
                extra.append((2, e))
        if (da, db, dz) == (0, 0, 0):
            for d in range(1, depth):
                landed(3, d - 1, first4 + d - 1)
                extra.append((3, d - 1))
        add(k, place.block(da, db, dz), extra, final=(da, db, dz) == (0, 0, 0))
        source = lambda data, bufs: bufs[0].at[k]
        if db:
            e = (db - 1) * side * depth + da * depth + dz
            push(source, 1, e, place.device(db=db), first2 + e)
        elif da:
            e = (da - 1) * depth + dz
            push(source, 2, e, place.device(da=da), first3 + e)
        elif dz:
            push(source, 3, dz - 1, place.device(dz=dz), first4 + dz - 1)
    for copy in started:
        copy.wait_send()


def scatter_blocks(factors, column_terms):
    devices = lax.axis_size("dp") * lax.axis_size("fsdp")
    share, outer_share = D // devices, FF // devices
    bf16 = jnp.bfloat16
    if not kernels_fit():
        tok, d_query, d_keys, d_values, mixed, d_first, hidden, d_pre, act, d_second = factors
        pairs = ((tok, d_query), (tok, d_keys), (tok, d_values), (mixed, d_first), (hidden, d_pre))
        a_terms = [product(left, right).astype(bf16) for left, right in pairs]
        a_terms = jnp.concatenate(a_terms + [column_terms], 1).reshape(devices, share, -1)
        b_terms = product(act, d_second).astype(bf16).reshape(devices, outer_share, D)
        return tuple(
            lax.psum_scatter(v, ("dp", "fsdp"), scatter_dimension=0, tiled=True)[0].astype(
                jnp.float32
            )
            for v in (a_terms, b_terms)
        )
    side, depth = math.isqrt(lax.axis_size("dp")), lax.axis_size("fsdp") // 2
    half = side * side * depth
    counts = (half, (side - 1) * side * depth, (side - 1) * depth, depth - 1)
    vmem = pl.BlockSpec(memory_space=pltpu.VMEM)
    shapes = ((share, 4 * D + FF + LANES), (outer_share, D))
    return pl.pallas_call(
        functools.partial(scatter_kernel, side, depth),
        name="scatter_blocks",
        out_shape=tuple(jax.ShapeDtypeStruct(v, jnp.float32) for v in shapes),
        in_specs=[vmem] * 11,
        out_specs=(vmem,) * 2,
        scratch_shapes=[pltpu.VMEM((devices,) + v, bf16) for v in shapes]
        + [pltpu.VMEM((max(n, 1),) + v, bf16) for v in shapes for n in counts]
        + [pltpu.SemaphoreType.DMA((2, devices)), pltpu.SemaphoreType.DMA((2, devices))],
        compiler_params=pltpu.CompilerParams(
            collective_id=1, has_side_effects=True, vmem_limit_bytes=52 * 2**20
        ),
    )(*factors, column_terms.reshape(devices, share, LANES))


def shards(
    tokens,
    lengths,
    cotangent,
    query_weight,
    query_bias,
    key_weight,
    value_weight,
    value_bias,
    out_weight,
    out_bias,
    norm1_gain,
    norm1_shift,
    inner_weight,
    inner_bias,
    outer_weight,
    outer_bias,
    norm2_gain,
    norm2_shift,
):
    bf16 = jnp.bfloat16
    length = lengths[0]
    share = query_weight.shape[0]
    wide = FF // D
    devices = lax.axis_size("dp") * lax.axis_size("fsdp")
    start = 4 * D + FF

    def columns(vectors, long_one):
        flat = jnp.concatenate(list(vectors) + [long_one.reshape(-1, wide).T.reshape(-1)])
        side_by_side = flat.reshape(len(vectors) + wide, -1)
        padding = LANES - side_by_side.shape[0]
        return jnp.pad(side_by_side.astype(bf16), ((0, padding), (0, 0))).T

    vector_block = columns(
        [
            query_bias,
            value_bias,
            out_bias,
            norm1_gain,
            norm1_shift,
            outer_bias,
            norm2_gain,
            norm2_shift,
        ],
        inner_bias,
    )
    every, outer = gather_blocks(
        [query_weight, key_weight, value_weight, out_weight, inner_weight, vector_block],
        outer_weight,
    )
    every = every.reshape(-1, every.shape[-1])
    vectors = every[:, start:].T

    whole = (
        every[:, 0:D],
        vectors[0],
        every[:, D : 2 * D],
        every[:, 2 * D : 3 * D],
        vectors[1],
        every[:, 3 * D : 4 * D],
        vectors[2],
        vectors[3],
        vectors[4],
        every[:, 4 * D : start],
        vectors[8 : 8 + wide].T.reshape(-1),
        outer.reshape(FF, D),
        vectors[5],
        vectors[6],
        vectors[7],
    )
    layer_out, saved = forward_pass(tokens, length, whole)
    grad_tokens, sums, factors = backward_pass(tokens, cotangent, length, whole, saved)
    factor = 1.0 / jnp.sqrt(jnp.float32(tokens.shape[0] * devices))
    column_terms = columns([sums[i] for i in (0, 1, 2, 3, 4, 6, 7, 8)], sums[5])
    owned, owned_outer = scatter_blocks(factors, column_terms)
    owned = owned * factor
    owned_vectors = owned[:, start:].T

    return (
        layer_out,
        grad_tokens,
        owned[:, 0:D],
        owned_vectors[0],
        owned[:, D : 2 * D],
        owned[:, 2 * D : 3 * D],
        owned_vectors[1],
        owned[:, 3 * D : 4 * D],
        owned_vectors[2],
        owned_vectors[3],
        owned_vectors[4],
        owned[:, 4 * D : start],
        owned_vectors[8 : 8 + wide].T.reshape(-1),
        owned_outer * factor,
        owned_vectors[5],
        owned_vectors[6],
        owned_vectors[7],
    )


def solution(mesh):
    placed = (
        P(("dp", "fsdp"), None),
        P(("dp", "fsdp")),
        P(("dp", "fsdp"), None),
        P(("dp", "fsdp"), None),
        P(("dp", "fsdp")),
        P(("dp", "fsdp"), None),
        P(("dp", "fsdp"), None),
        P(("dp", "fsdp")),
        P(("dp", "fsdp"), None),
        P(("dp", "fsdp")),
        P(("dp", "fsdp")),
        P(("dp", "fsdp")),
        P(("dp", "fsdp"), None),
        P(("dp", "fsdp")),
        P(("dp", "fsdp"), None),
        P(("dp", "fsdp")),
        P(("dp", "fsdp")),
        P(("dp", "fsdp")),
    )
    return jax.shard_map(
        shards,
        mesh=mesh,
        in_specs=placed,
        out_specs=(
            P(("dp", "fsdp"), None),
            P(("dp", "fsdp"), None),
            P(("dp", "fsdp"), None),
            P(("dp", "fsdp")),
            P(("dp", "fsdp"), None),
            P(("dp", "fsdp"), None),
            P(("dp", "fsdp")),
            P(("dp", "fsdp"), None),
            P(("dp", "fsdp")),
            P(("dp", "fsdp")),
            P(("dp", "fsdp")),
            P(("dp", "fsdp"), None),
            P(("dp", "fsdp")),
            P(("dp", "fsdp"), None),
            P(("dp", "fsdp")),
            P(("dp", "fsdp")),
            P(("dp", "fsdp")),
        ),
        check_vma=False,
    )
```

```python
import functools
import math

import jax
import jax.numpy as jnp
from jax import lax
from jax.experimental import pallas as pl
from jax.experimental.pallas import tpu as pltpu
from jax.sharding import PartitionSpec as P

D = 768
HEADS = 12
HEAD_DIM = 64
FF = 3072


NORM_EPS = 1e-12
ATTN_SCALE = 0.125


def layer_norm(summed, gain, shift):
    center = summed - jnp.mean(summed, -1, keepdims=True)
    rstd = lax.rsqrt(jnp.mean(center * center, -1, keepdims=True) + NORM_EPS)
    normed = center * rstd
    return (normed * gain.astype(jnp.float32) + shift.astype(jnp.float32), normed, rstd)


def norm_back(grad_in, normed, rstd, gain):
    scaled = grad_in * gain.astype(jnp.float32)
    return rstd * (
        scaled
        - jnp.mean(scaled, -1, keepdims=True)
        - normed * jnp.mean(scaled * normed, -1, keepdims=True)
    )


def gelu_parts(pre):
    cdf = 0.5 * (1.0 + jax.scipy.special.erf(pre * 0.7071067811865476))
    slope = cdf + pre * jnp.exp(-0.5 * pre * pre) * 0.3989422804014327
    return (pre * cdf, slope)


def heads_of(rows):
    return rows.reshape(rows.shape[0], HEADS, HEAD_DIM)


def get_scores(query, keys, length):
    scores = (
        jnp.einsum(
            "qhd,khd->hqk", heads_of(query), heads_of(keys), preferred_element_type=jnp.float32
        )
        * ATTN_SCALE
    )
    valid = jnp.arange(scores.shape[-1]) < length
    return jnp.where(valid[None, None, :], scores, -1e30)


def forward_pass(tokens, length, weights):
    (
        query_weight,
        query_bias,
        key_weight,
        value_weight,
        value_bias,
        out_weight,
        out_bias,
        norm1_gain,
        norm1_shift,
        inner_weight,
        inner_bias,
        outer_weight,
        outer_bias,
        norm2_gain,
        norm2_shift,
    ) = weights
    f32 = jnp.float32
    bf16 = jnp.bfloat16
    query = (
        jnp.dot(tokens, query_weight, preferred_element_type=f32) + query_bias.astype(f32)
    ).astype(bf16)
    keys = jnp.dot(tokens, key_weight, preferred_element_type=f32).astype(bf16)
    values = (
        jnp.dot(tokens, value_weight, preferred_element_type=f32) + value_bias.astype(f32)
    ).astype(bf16)
    scores = get_scores(query, keys, length)
    top = jnp.max(scores, -1)
    lse = top + jnp.log(jnp.sum(jnp.exp(scores - top[..., None]), -1))
    probs_b = jnp.exp(scores - lse[..., None]).astype(bf16)
    mixed = jnp.einsum("hqk,khd->qhd", probs_b, heads_of(values), preferred_element_type=f32)
    mixed = mixed.reshape(tokens.shape[0], -1).astype(bf16)
    first_sum = (
        tokens.astype(f32)
        + jnp.dot(mixed, out_weight, preferred_element_type=f32)
        + out_bias.astype(f32)
    )
    hidden, normed_one, rstd_one = layer_norm(first_sum, norm1_gain, norm1_shift)
    hidden_b = hidden.astype(bf16)
    pre = jnp.dot(hidden_b, inner_weight, preferred_element_type=f32) + inner_bias.astype(f32)
    act, slope = gelu_parts(pre)
    act_b = act.astype(bf16)
    second_sum = (
        hidden + jnp.dot(act_b, outer_weight, preferred_element_type=f32) + outer_bias.astype(f32)
    )
    layer_out, normed_two, rstd_two = layer_norm(second_sum, norm2_gain, norm2_shift)
    saved = (
        query,
        keys,
        values,
        lse,
        mixed,
        normed_one,
        rstd_one,
        hidden_b,
        slope,
        act_b,
        normed_two,
        rstd_two,
    )
    return (layer_out, saved)


def backward_pass(tokens, cotangent, length, weights, saved):
    (
        query_weight,
        query_bias,
        key_weight,
        value_weight,
        value_bias,
        out_weight,
        out_bias,
        norm1_gain,
        norm1_shift,
        inner_weight,
        inner_bias,
        outer_weight,
        outer_bias,
        norm2_gain,
        norm2_shift,
    ) = weights
    (
        query,
        keys,
        values,
        lse,
        mixed,
        normed_one,
        rstd_one,
        hidden_b,
        slope,
        act_b,
        normed_two,
        rstd_two,
    ) = saved
    f32 = jnp.float32
    bf16 = jnp.bfloat16
    d_second = norm_back(cotangent, normed_two, rstd_two, norm2_gain)
    d_second_b = d_second.astype(bf16)
    d_pre = jnp.dot(d_second_b, outer_weight.T, preferred_element_type=f32) * slope
    d_pre_b = d_pre.astype(bf16)
    d_hidden = d_second + jnp.dot(d_pre_b, inner_weight.T, preferred_element_type=f32)
    d_first = norm_back(d_hidden, normed_one, rstd_one, norm1_gain)
    d_first_b = d_first.astype(bf16)
    d_mixed = jnp.dot(d_first_b, out_weight.T, preferred_element_type=f32).astype(bf16)
    again = jnp.exp(get_scores(query, keys, length) - lse[..., None])
    again_b = again.astype(bf16)
    d_probs = jnp.einsum(
        "qhd,khd->hqk", heads_of(d_mixed), heads_of(values), preferred_element_type=f32
    )
    d_values_f = jnp.einsum(
        "hqk,qhd->khd", again_b, heads_of(d_mixed), preferred_element_type=f32
    ).reshape(tokens.shape[0], -1)
    delta = jnp.sum(again * d_probs, -1, keepdims=True)
    d_scores = (again * (d_probs - delta) * ATTN_SCALE).astype(bf16)
    d_query_f = jnp.einsum(
        "hqk,khd->qhd", d_scores, heads_of(keys), preferred_element_type=f32
    ).reshape(tokens.shape[0], -1)
    d_keys_f = jnp.einsum(
        "hqk,qhd->khd", d_scores, heads_of(query), preferred_element_type=f32
    ).reshape(tokens.shape[0], -1)
    d_query = d_query_f.astype(bf16)
    d_keys = d_keys_f.astype(bf16)
    d_values = d_values_f.astype(bf16)
    grad_tokens = (
        d_first
        + jnp.dot(d_query, query_weight.T, preferred_element_type=f32)
        + jnp.dot(d_keys, key_weight.T, preferred_element_type=f32)
        + jnp.dot(d_values, value_weight.T, preferred_element_type=f32)
    )
    small = (
        jnp.sum(d_query_f, 0),
        jnp.sum(d_values_f, 0),
        jnp.sum(d_first, 0),
        jnp.sum(d_hidden * normed_one, 0),
        jnp.sum(d_hidden, 0),
        jnp.sum(d_pre, 0),
        jnp.sum(d_second, 0),
        jnp.sum(cotangent * normed_two, 0),
        jnp.sum(cotangent, 0),
    )
    factors = (
        tokens,
        d_query,
        d_keys,
        d_values,
        mixed,
        d_first_b,
        hidden_b,
        d_pre_b,
        act_b,
        d_second_b,
    )
    return (grad_tokens, small, factors)


MESH = pl.DeviceIdType.MESH
LANES = 128


class Place:
    def __init__(self, side, depth):
        self.side, self.depth = side, depth
        dp, fsdp = lax.axis_index("dp"), lax.axis_index("fsdp")
        self.c = fsdp % 2
        self.z = fsdp // 2
        row, col = dp // side, dp % side
        self.a = (1 - self.c) * col + self.c * row
        self.b = (1 - self.c) * row + self.c * col
        self.dp = dp

    def column(self, a, b, c):
        return (1 - c) * (b * self.side + a) + c * (a * self.side + b)

    def device(self, da=0, db=0, dz=0):
        a, b = (self.a + da) % self.side, (self.b + db) % self.side
        z = (self.z + dz) % self.depth
        return (self.column(a, b, self.c), z * 2 + self.c)

    def block(self, da, db, dz):
        dp, fsdp = self.device(da, db, dz)
        return dp * (2 * self.depth) + fsdp

    def sibling(self):
        return (self.dp, self.z * 2 + 1 - self.c)

    def sibling_block(self, da, db, dz):
        c = 1 - self.c
        a, b = (self.b + da) % self.side, (self.a + db) % self.side
        z = (self.z + dz) % self.depth
        return self.column(a, b, c) * (2 * self.depth) + z * 2 + c


def greet(place):
    barrier = pltpu.get_barrier_semaphore()
    others = [place.device(da=k) for k in range(1, place.side)]
    others += [place.device(db=k) for k in range(1, place.side)]
    others += [place.device(dz=k) for k in range(1, place.depth)]
    others.append(place.sibling())
    for other in others:
        pl.semaphore_signal(barrier, inc=1, device_id=other, device_id_type=MESH)
    return len(others)


def gather_kernel(side, depth, parts, *refs):
    part_refs = refs[:parts]
    b_ref, a_out, b_out, a_ref, keep, sent, got = refs[parts:]
    place = Place(side, depth)
    greeted = greet(place)
    at = 0
    for part in part_refs:
        a_ref[0, :, at : at + part.shape[1]] = part[...]
        at += part.shape[1]
    pl.semaphore_wait(pltpu.get_barrier_semaphore(), greeted)
    pairs = ((a_ref, a_out), (b_ref, b_out))
    me = place.block(0, 0, 0)
    own = [
        pltpu.make_async_copy(src.at[0], dst.at[me], keep.at[i])
        for i, (src, dst) in enumerate(pairs)
    ]
    for copy in own:
        copy.start()
    started = []
    counts = [0, 0]
    half = side * side * depth

    def slot(da, db, dz):
        return (db * side + da) * depth + dz

    def push(piece, source, device, at, sem_at):
        for i, (src, dst) in [(piece, pairs[piece])]:
            origin = src.at[0] if source is None else dst.at[source]
            copy = pltpu.make_async_remote_copy(
                src_ref=origin,
                dst_ref=dst.at[at],
                send_sem=sent.at[i, counts[i]],
                recv_sem=got.at[i, sem_at],
                device_id=device,
                device_id_type=MESH,
            )
            copy.start()
            counts[i] += 1
            started.append(copy)

    def landed(piece, index, sem_at):
        dst = pairs[piece][1]
        pltpu.make_async_copy(dst.at[index], dst.at[index], got.at[piece, sem_at]).wait()

    def spread(piece, source, da, db, dz):
        index = place.block(da, db, dz)
        if da == 0 and db == 0:
            for k in range(1, side):
                push(piece, source, place.device(da=k), index, slot((side - k) % side, 0, dz))
        if db == 0:
            for k in range(1, side):
                push(piece, source, place.device(db=k), index, slot(da, (side - k) % side, dz))
        push(piece, source, place.sibling(), index, half + slot(da, db, dz))

    for piece in range(2):
        for dz in range(1, depth):
            push(piece, None, place.device(dz=dz), me, slot(0, 0, depth - dz))
        spread(piece, None, 0, 0, 0)
    near = sorted(range(1, depth), key=lambda k: min(k, depth - k))
    steps = []
    for rank, dz in enumerate([0] + near):
        for db in range(side):
            for da in range(side):
                if (da, db, dz) != (0, 0, 0):
                    steps.append((rank + (da > 0) + 2 * (db > 0), da, db, dz))
    for _, da, db, dz in sorted(steps):
        index = place.block(da, db, dz)
        for piece in range(2):
            landed(piece, index, slot(da, db, dz))
            spread(piece, index, da, db, dz)
    for db in range(side):
        for da in range(side):
            for dz in range(depth):
                for piece in range(2):
                    landed(piece, place.sibling_block(da, db, dz), half + slot(da, db, dz))
    for copy in own:
        copy.wait()
    for copy in started:
        copy.wait_send()


def kernels_fit():
    side = math.isqrt(lax.axis_size("dp"))
    devices = lax.axis_size("dp") * lax.axis_size("fsdp")
    return side * side == lax.axis_size("dp") and lax.axis_size("fsdp") % 2 == 0 and devices <= 32


def gather_blocks(a_parts, b_block):
    if not kernels_fit():
        a_block = jnp.concatenate(a_parts, 1)
        return tuple(lax.all_gather(v, ("dp", "fsdp"), axis=0) for v in (a_block, b_block))
    side, depth = math.isqrt(lax.axis_size("dp")), lax.axis_size("fsdp") // 2
    devices = 2 * side * side * depth
    rows, lanes = b_block.shape[0], sum(v.shape[1] for v in a_parts)
    share = a_parts[0].shape[0]
    dtype = b_block.dtype
    anywhere = pl.BlockSpec(memory_space=pl.ANY)
    vmem = pl.BlockSpec(memory_space=pltpu.VMEM)
    return pl.pallas_call(
        functools.partial(gather_kernel, side, depth, len(a_parts)),
        name="gather_blocks",
        out_shape=(
            jax.ShapeDtypeStruct((devices, share, lanes), dtype),
            jax.ShapeDtypeStruct((devices, rows, D), dtype),
        ),
        in_specs=[vmem] * len(a_parts) + [anywhere],
        out_specs=(anywhere,) * 2,
        scratch_shapes=[
            pltpu.VMEM((1, share, lanes), dtype),
            pltpu.SemaphoreType.DMA((2,)),
            pltpu.SemaphoreType.DMA((2, devices)),
            pltpu.SemaphoreType.DMA((2, devices)),
        ],
        compiler_params=pltpu.CompilerParams(collective_id=0, has_side_effects=True),
    )(*a_parts, b_block[None])


def product(left, right):
    return lax.dot_general(
        left, right, (((0,), (0,)), ((), ())), preferred_element_type=jnp.float32
    )


def fill(factors, column_ref, a_in, b_in):
    tok, d_query, d_keys, d_values, mixed, d_first, hidden, d_pre, act, d_second = factors
    share, outer_share = a_in.shape[1], b_in.shape[1]
    part = D // 2
    pairs = [(tok, d_query, 0), (tok, d_keys, 0), (tok, d_values, 0), (mixed, d_first, 0)]
    pairs += [(hidden, d_pre, j * D) for j in range(FF // D)]
    for at, (left, right, lane) in enumerate(pairs):
        for m in range(0, D, part):
            block = product(left[:, m : m + part], right[:, lane : lane + D])
            block = block.reshape(part // share, share, D).astype(jnp.bfloat16)
            a_in[m // share : (m + part) // share, :, at * D : (at + 1) * D] = block
    a_in[:, :, len(pairs) * D :] = column_ref[...]
    for m in range(0, FF, part):
        block = product(act[:, m : m + part], d_second[...])
        block = block.reshape(part // outer_share, outer_share, D).astype(jnp.bfloat16)
        b_in[m // outer_share : (m + part) // outer_share] = block


def scatter_kernel(side, depth, *refs):
    factors, column_ref, a_out, b_out = refs[0:10], refs[10], refs[11], refs[12]
    a_in, b_in = refs[13:15]
    a_bufs, b_bufs = refs[15:19], refs[19:23]
    sent, got = refs[23:25]
    place = Place(side, depth)
    greeted = greet(place)
    fill(factors, column_ref, a_in, b_in)
    pl.semaphore_wait(pltpu.get_barrier_semaphore(), greeted)
    started = []
    half = side * side * depth
    first2 = half
    first3 = first2 + (side - 1) * side * depth
    first4 = first3 + (side - 1) * depth
    groups = ((a_in, a_bufs, a_out), (b_in, b_bufs, b_out))

    def slot(da, db, dz):
        return (db * side + da) * depth + dz

    def push(pick_source, level, at, device, sem_at):
        for i, (data, bufs, _) in enumerate(groups):
            copy = pltpu.make_async_remote_copy(
                src_ref=pick_source(data, bufs),
                dst_ref=bufs[level].at[at],
                send_sem=sent.at[i, len(started) // 2],
                recv_sem=got.at[i, sem_at],
                device_id=device,
                device_id_type=MESH,
            )
            copy.start()
            started.append(copy)

    def landed(level, at, sem_at):
        for i, (_, bufs, _) in enumerate(groups):
            ref = bufs[level].at[at]
            pltpu.make_async_copy(ref, ref, got.at[i, sem_at]).wait()

    def add(k, block, extra, final=False):
        for data, bufs, out in groups:
            rows, lanes = data.shape[1:]
            wide = lanes > D
            step = lanes // 7 if wide else rows // 6
            count = 7 if wide else 6

            def body(n, _):
                if wide:
                    at = (slice(None), pl.ds(pl.multiple_of(n * step, LANES), step))
                else:
                    at = (pl.ds(pl.multiple_of(n * step, 16), step), slice(None))
                total = bufs[0][(k,) + at].astype(jnp.float32)
                total += data[(block,) + at].astype(jnp.float32)
                for level, e in extra:
                    total += bufs[level][(e,) + at].astype(jnp.float32)
                if final:
                    out[at] = total
                else:
                    bufs[0][(k,) + at] = total.astype(jnp.bfloat16)
                return 0

            lax.fori_loop(0, count, body, 0)

    order = [
        (da, db, dz)
        for db in range(side - 1, -1, -1)
        for da in range(side - 1, -1, -1)
        for dz in range(depth - 1, -1, -1)
    ]
    for da, db, dz in order:
        index = place.sibling_block(da, db, dz)
        k = slot(da, db, dz)
        push(lambda data, bufs: data.at[index], 0, k, place.sibling(), k)
    for da, db, dz in order:
        k = slot(da, db, dz)
        landed(0, k, k)
        extra = []
        if db == 0:
            for d in range(1, side):
                e = (d - 1) * side * depth + da * depth + dz
                landed(1, e, first2 + e)
                extra.append((1, e))
        if db == 0 and da == 0:
            for d in range(1, side):
                e = (d - 1) * depth + dz
                landed(2, e, first3 + e)
                extra.append((2, e))
        if (da, db, dz) == (0, 0, 0):
            for d in range(1, depth):
                landed(3, d - 1, first4 + d - 1)
                extra.append((3, d - 1))
        add(k, place.block(da, db, dz), extra, final=(da, db, dz) == (0, 0, 0))
        source = lambda data, bufs: bufs[0].at[k]
        if db:
            e = (db - 1) * side * depth + da * depth + dz
            push(source, 1, e, place.device(db=db), first2 + e)
        elif da:
            e = (da - 1) * depth + dz
            push(source, 2, e, place.device(da=da), first3 + e)
        elif dz:
            push(source, 3, dz - 1, place.device(dz=dz), first4 + dz - 1)
    for copy in started:
        copy.wait_send()


def scatter_blocks(factors, column_terms):
    devices = lax.axis_size("dp") * lax.axis_size("fsdp")
    share, outer_share = D // devices, FF // devices
    bf16 = jnp.bfloat16
    if not kernels_fit():
        tok, d_query, d_keys, d_values, mixed, d_first, hidden, d_pre, act, d_second = factors
        pairs = ((tok, d_query), (tok, d_keys), (tok, d_values), (mixed, d_first), (hidden, d_pre))
        a_terms = [product(left, right).astype(bf16) for left, right in pairs]
        a_terms = jnp.concatenate(a_terms + [column_terms], 1).reshape(devices, share, -1)
        b_terms = product(act, d_second).astype(bf16).reshape(devices, outer_share, D)
        return tuple(
            lax.psum_scatter(v, ("dp", "fsdp"), scatter_dimension=0, tiled=True)[0].astype(
                jnp.float32
            )
            for v in (a_terms, b_terms)
        )
    side, depth = math.isqrt(lax.axis_size("dp")), lax.axis_size("fsdp") // 2
    half = side * side * depth
    counts = (half, (side - 1) * side * depth, (side - 1) * depth, depth - 1)
    vmem = pl.BlockSpec(memory_space=pltpu.VMEM)
    shapes = ((share, 4 * D + FF + LANES), (outer_share, D))
    return pl.pallas_call(
        functools.partial(scatter_kernel, side, depth),
        name="scatter_blocks",
        out_shape=tuple(jax.ShapeDtypeStruct(v, jnp.float32) for v in shapes),
        in_specs=[vmem] * 11,
        out_specs=(vmem,) * 2,
        scratch_shapes=[pltpu.VMEM((devices,) + v, bf16) for v in shapes]
        + [pltpu.VMEM((max(n, 1),) + v, bf16) for v in shapes for n in counts]
        + [pltpu.SemaphoreType.DMA((2, devices)), pltpu.SemaphoreType.DMA((2, devices))],
        compiler_params=pltpu.CompilerParams(
            collective_id=1, has_side_effects=True, vmem_limit_bytes=52 * 2**20
        ),
    )(*factors, column_terms.reshape(devices, share, LANES))


def shards(
    tokens,
    lengths,
    cotangent,
    query_weight,
    query_bias,
    key_weight,
    value_weight,
    value_bias,
    out_weight,
    out_bias,
    norm1_gain,
    norm1_shift,
    inner_weight,
    inner_bias,
    outer_weight,
    outer_bias,
    norm2_gain,
    norm2_shift,
):
    bf16 = jnp.bfloat16
    length = lengths[0]
    share = query_weight.shape[0]
    wide = FF // D
    devices = lax.axis_size("dp") * lax.axis_size("fsdp")
    start = 4 * D + FF

    def columns(vectors, long_one):
        flat = jnp.concatenate(list(vectors) + [long_one.reshape(-1, wide).T.reshape(-1)])
        side_by_side = flat.reshape(len(vectors) + wide, -1)
        padding = LANES - side_by_side.shape[0]
        return jnp.pad(side_by_side.astype(bf16), ((0, padding), (0, 0))).T

    vector_block = columns(
        [
            query_bias,
            value_bias,
            out_bias,
            norm1_gain,
            norm1_shift,
            outer_bias,
            norm2_gain,
            norm2_shift,
        ],
        inner_bias,
    )
    every, outer = gather_blocks(
        [query_weight, key_weight, value_weight, out_weight, inner_weight, vector_block],
        outer_weight,
    )
    every = every.reshape(-1, every.shape[-1])
    vectors = every[:, start:].T

    whole = (
        every[:, 0:D],
        vectors[0],
        every[:, D : 2 * D],
        every[:, 2 * D : 3 * D],
        vectors[1],
        every[:, 3 * D : 4 * D],
        vectors[2],
        vectors[3],
        vectors[4],
        every[:, 4 * D : start],
        vectors[8 : 8 + wide].T.reshape(-1),
        outer.reshape(FF, D),
        vectors[5],
        vectors[6],
        vectors[7],
    )
    layer_out, saved = forward_pass(tokens, length, whole)
    grad_tokens, sums, factors = backward_pass(tokens, cotangent, length, whole, saved)
    factor = 1.0 / jnp.sqrt(jnp.float32(tokens.shape[0] * devices))
    column_terms = columns([sums[i] for i in (0, 1, 2, 3, 4, 6, 7, 8)], sums[5])
    owned, owned_outer = scatter_blocks(factors, column_terms)
    owned = owned * factor
    owned_vectors = owned[:, start:].T

    return (
        layer_out,
        grad_tokens,
        owned[:, 0:D],
        owned_vectors[0],
        owned[:, D : 2 * D],
        owned[:, 2 * D : 3 * D],
        owned_vectors[1],
        owned[:, 3 * D : 4 * D],
        owned_vectors[2],
        owned_vectors[3],
        owned_vectors[4],
        owned[:, 4 * D : start],
        owned_vectors[8 : 8 + wide].T.reshape(-1),
        owned_outer * factor,
        owned_vectors[5],
        owned_vectors[6],
        owned_vectors[7],
    )


def solution(mesh):
    placed = (
        P(("dp", "fsdp"), None),
        P(("dp", "fsdp")),
        P(("dp", "fsdp"), None),
        P(("dp", "fsdp"), None),
        P(("dp", "fsdp")),
        P(("dp", "fsdp"), None),
        P(("dp", "fsdp"), None),
        P(("dp", "fsdp")),
        P(("dp", "fsdp"), None),
        P(("dp", "fsdp")),
        P(("dp", "fsdp")),
        P(("dp", "fsdp")),
        P(("dp", "fsdp"), None),
        P(("dp", "fsdp")),
        P(("dp", "fsdp"), None),
        P(("dp", "fsdp")),
        P(("dp", "fsdp")),
        P(("dp", "fsdp")),
    )
    return jax.shard_map(
        shards,
        mesh=mesh,
        in_specs=placed,
        out_specs=(
            P(("dp", "fsdp"), None),
            P(("dp", "fsdp"), None),
            P(("dp", "fsdp"), None),
            P(("dp", "fsdp")),
            P(("dp", "fsdp"), None),
            P(("dp", "fsdp"), None),
            P(("dp", "fsdp")),
            P(("dp", "fsdp"), None),
            P(("dp", "fsdp")),
            P(("dp", "fsdp")),
            P(("dp", "fsdp")),
            P(("dp", "fsdp"), None),
            P(("dp", "fsdp")),
            P(("dp", "fsdp"), None),
            P(("dp", "fsdp")),
            P(("dp", "fsdp")),
            P(("dp", "fsdp")),
        ),
        check_vma=False,
    )
```
